256 devices in a mesh: pop: 32 (over z, y), wa: 8 (over x, core).
Axes of the slice: x: 4, y: 4, z: 8, core: 2. Of those that a mesh axis runs over, the one named last changes fastest.
Arguments:
- inputs: bfloat16 [16384, 4096], P('pop'), may hold values from -6 to 6
- noise_left: bfloat16 [16384, 4096], P('pop'), may hold values from -6 to 6
- noise_right: bfloat16 [16384, 8192], P('pop', 'wa'), may hold values from -6 to 6
- reward_probe: float32 [8192], P('wa'), may hold values from -6 to 6
- scores: int32 [16384], P('pop'), may hold values from 0 to 31
- master: float32 [4096, 8192], P('pop', 'wa'), may hold values from -0.1 to 0.1, as said below
Outputs:
- fitness: float32 [16384], P('pop')
- update: float32 [4096, 8192], P('pop', 'wa')
- new_master: float32 [4096, 8192], P('pop', 'wa')
- new_copy: bfloat16 [4096, 8192], P('pop', 'wa')
The draws below stay inside these ranges and needn't reach their ends.
Inputs may be any that keep to these rules, and one draw needn't show every extreme that they name: master's entries are values that bfloat16 represents exactly.
All inputs are finite; a program needn't handle non-finite values.
Results may differ from the reference program's by a relative error of at most 0.0037.
Values may be sent and summed in bfloat16 or wider, within the bound.
No kernel may reach another device: no remote copies, remote signals or barrier semaphores. Data moves between devices by JAX's collectives and lax.ppermute only.
A program may use at most 128 MiB of HBM per device.

```python
import math
import jax
import jax.numpy as jnp
from jax import lax

D = 4096
F = 8192
POP_DEV = 512
POPULATION = 16384


def draw_master(key, part):
    key = jax.random.fold_in(key, 7)
    values = jnp.clip(jax.random.normal(key, (D, F), jnp.float32), -6.0, 6.0)
    values = values * (1.0 / 64.0)
    values = jnp.clip(values, -0.09, 0.09)
    return values.astype(jnp.bfloat16).astype(jnp.float32)


def touch_ends(result, own_key, smallest, high):
    shape = result.shape
    place = [jax.random.randint(jax.random.fold_in(own_key, axis), (), 0, shape[axis]) for axis in range(len(shape))]
    result = result.at[tuple(place)].set(smallest)
    longest = shape.index(max(shape))
    place[longest] = (place[longest] + 1) % shape[longest]
    return result.at[tuple(place)].set(high)


def strengthened(values, rng, source, target, parts, factor):
    owner, partner = [(jnp.arange(values.shape[dim]) // (values.shape[dim] // parts)).reshape([-1 if axis == dim else 1 for axis in range(values.ndim)]) for dim in (source, target)]
    chosen = jax.random.permutation(rng, parts)[partner]
    strong = (owner == chosen) | (owner == (partner + parts // 2) % parts)
    return jnp.where(strong, factor * values, values)


def level_of(stream_key, dims, pieces, least, high):
    level = 1.0
    for position, parts in pieces:
        steps = jax.random.uniform(jax.random.fold_in(jax.random.fold_in(stream_key, 6), position), (parts,), jnp.float32, least / len(pieces), high / len(pieces))
        level = level * jnp.repeat(jnp.exp(steps), dims[position] // parts).reshape((-1,) + (1,) * (len(dims) - 1 - position))
    return level


def centred(rng, dims, deviation, most, pieces=(), dtype=jnp.bfloat16):
    level = level_of(rng, dims, pieces, -0.22, 0.18) if pieces else 1.0
    array = jax.random.normal(rng, dims, jnp.float32) * deviation * level
    return jnp.minimum(jnp.maximum(array, -most), most).astype(dtype)


def bell_draw_with(stream_key, dims, deviation, most, split, heavy, held_as=jnp.bfloat16):
    array = deviation * jax.random.normal(stream_key, dims, jnp.float32)
    if split:
        array = array * level_of(stream_key, dims, split, -0.22, 0.18)
    return jnp.clip(strengthened(array, jax.random.fold_in(stream_key, 3), *heavy), -most, most).astype(held_as)


def setup_inputs(seed: int = 0) -> dict:
    splits = jax.random.split(jax.random.key(seed), 7)
    return {
        "inputs": centred(splits[0], (POPULATION, D), 1.0, 6.0, ((0, 32),)),
        "noise_left": bell_draw_with(splits[1], (POPULATION, D), 1.0, 6.0, ((0, 32),), (0, 1, 32, 2.75)),
        "noise_right": centred(splits[2], (POPULATION, F), 1.0, 6.0, ((0, 32), (1, 8))),
        "reward_probe": centred(splits[3], (F,), 1.0, 6.0, ((0, 8),), jnp.float32),
        "scores": touch_ends(jax.random.randint(splits[4], (POPULATION,), 0, 32), jax.random.fold_in(splits[4], 1), 0, 31).astype(jnp.int32),
        "master": draw_master(jax.random.fold_in(splits[6], 71), 0),
    }


noise_scale = 0.5
learn_rate = 0.01
epsilon = 1e-05

def reference(inputs, noise_left, noise_right, reward_probe, scores, master):
    weight_half = master.astype(jnp.bfloat16)
    population = inputs.shape[0]
    groups = population // POP_DEV

    def member_rewards(blocks):
        rows, left, right = blocks
        base_out = jnp.dot(rows, weight_half, preferred_element_type=jnp.float32)
        projected = lax.optimization_barrier(jnp.sum(rows.astype(jnp.float32) * left.astype(jnp.float32), axis=1)) / math.sqrt(D)
        outputs = base_out + noise_scale * projected[:, None] * right.astype(jnp.float32)
        return jnp.dot(jnp.tanh(outputs), reward_probe, precision=lax.Precision.HIGHEST) / math.sqrt(F)
    reward = lax.map(member_rewards, (inputs.reshape(groups, POP_DEV, D), noise_left.reshape(groups, POP_DEV, D), noise_right.reshape(groups, POP_DEV, F))).reshape(population)
    raw_fitness = reward + scores.astype(jnp.float32) / 16.0
    center = jnp.sum(raw_fitness) / population
    spread = jnp.sum(raw_fitness * raw_fitness) / population - center * center
    fitness = (raw_fitness - center) * lax.rsqrt(spread + epsilon)
    scaled = ((fitness / math.sqrt(population))[:, None] * noise_right.astype(jnp.float32)).astype(jnp.bfloat16)
    update = lax.dot_general(noise_left, scaled, (((0,), (0,)), ((), ())), preferred_element_type=jnp.float32)
    new_master = master + learn_rate * update
    return (fitness, update, new_master, new_master.astype(jnp.bfloat16))
```

```python
import math

import jax
import jax.numpy as jnp
from jax import lax
from jax.experimental import pallas as pl
from jax.experimental.pallas import tpu as pltpu
from jax.sharding import PartitionSpec as P

D = 4096
F = 8192
NZ, NY, NX = 8, 4, 4
MEMBERS = 512
SHARE = 64

noise_scale = 0.5
learn_rate = 0.01
epsilon = 1e-05

bf16 = jnp.bfloat16
f32 = jnp.float32


def move(value, dz, dy):
    pairs = [
        (z * NY + y, (z + dz) % NZ * NY + (y + dy) % NY)
        for z in range(NZ)
        for y in range(NY)
    ]
    return lax.ppermute(value, "pop", pairs)


def swap_pop(value, mask):
    return lax.ppermute(value, "pop", [(i, i ^ mask) for i in range(NZ * NY)])


def swap_wa(value, mask):
    return lax.ppermute(value, "wa", [(i, i ^ mask) for i in range(2 * NX)])


def move_x(value, dx):
    pairs = [
        (2 * x + c, 2 * ((x + dx) % NX) + c) for x in range(NX) for c in range(2)
    ]
    return lax.ppermute(value, "wa", pairs)


def z_gather(block):
    half = block.shape[0] // 2
    up1, down1 = move(block, -1, 0), move(block, 1, 0)
    up2, down2 = move(up1, -1, 0), move(down1, 1, 0)
    up3, down3 = move(up2, -1, 0), move(down2, 1, 0)
    up4, down4 = move(up3[:half], -1, 0), move(down3[half:], 1, 0)
    return [block, up1, up2, up3, jnp.concatenate([up4, down4]), down3, down2, down1]


def y_gather(block):
    return [block, move(block, 0, -1), move(block, 0, 2), move(block, 0, 1)]


def copy_inputs(place, source, by_y, by_z):
    by_y[...] = source[...]
    by_z[...] = source[...]


def relative_inputs(inputs, place):
    rows = inputs.shape[0]
    return pl.pallas_call(
        copy_inputs,
        grid_spec=pltpu.PrefetchScalarGridSpec(
            num_scalar_prefetch=1,
            grid=(NZ, NY),
            in_specs=[
                pl.BlockSpec(
                    (rows, 128),
                    lambda i, j, s: (0, lax.rem(s[0] + i, NZ) * NY + lax.rem(s[1] + j, NY)),
                )
            ],
            out_specs=[
                pl.BlockSpec((rows, 128), lambda i, j, s: (0, j * NZ + i)),
                pl.BlockSpec((rows, 128), lambda i, j, s: (0, i * NY + j)),
            ],
        ),
        out_shape=[jax.ShapeDtypeStruct((rows, D), bf16)] * 2,
        cost_estimate=pl.CostEstimate(
            flops=0, bytes_accessed=3 * rows * D * 2, transcendentals=0
        ),
    )(place, inputs)


def copy_block(place, source, target):
    target[0] = source[...]


def relative_left(noise_left, place):
    rows = noise_left.shape[0]
    return pl.pallas_call(
        copy_block,
        grid_spec=pltpu.PrefetchScalarGridSpec(
            num_scalar_prefetch=1,
            grid=(2, NZ),
            in_specs=[
                pl.BlockSpec((rows, 256), lambda h, i, s: (0, lax.rem(s[0] + i, NZ) * 2 + h))
            ],
            out_specs=pl.BlockSpec((1, rows, 256), lambda h, i, s: (h, 0, i)),
        ),
        out_shape=jax.ShapeDtypeStruct((2, rows, D // 2), bf16),
        cost_estimate=pl.CostEstimate(
            flops=0, bytes_accessed=2 * rows * D * 2, transcendentals=0
        ),
    )(place, noise_left)


def forward_dot(left, right):
    return jnp.dot(left, right, preferred_element_type=f32)


def update_dot(left, right):
    return lax.dot_general(
        left, right, (((0,), (0,)), ((), ())), preferred_element_type=f32
    )


def line_order(values, x, core):
    rest = values.shape[2:]
    split = values.reshape((3, NX, 2, SHARE) + rest)
    mine = lax.dynamic_index_in_dim(split, core, 2, keepdims=False)
    twice = jnp.concatenate([mine, mine], axis=1)
    turned = lax.dynamic_slice_in_dim(twice, x, NX, 1)
    return jnp.swapaxes(turned, 0, 1).reshape((3 * NX * SHARE,) + rest)


def shards(inputs, noise_left, noise_right, reward_probe, scores, master):
    population = MEMBERS * NZ * NY
    pop, wa = lax.axis_index("pop"), lax.axis_index("wa")
    z, y = pop // NY, pop % NY
    x, core = wa // 2, wa % 2
    half, parity = y // 2, y % 2
    place = jnp.stack([z, y]).astype(jnp.int32)

    weight = master.astype(bf16)
    first = jnp.concatenate(z_gather(weight[:, :512]))
    second = jnp.concatenate(y_gather(weight[:, 512:]))
    by_y, by_z = relative_inputs(inputs, place)
    out_first = sum(
        forward_dot(by_y[:, i * 1024 : (i + 1) * 1024], block)
        for i, block in enumerate(y_gather(first))
    )
    out_second = sum(
        forward_dot(by_z[:, i * 512 : (i + 1) * 512], block)
        for i, block in enumerate(z_gather(second))
    )

    left = relative_left(noise_left, place)
    share = lax.dynamic_slice_in_dim(left, wa * SHARE, SHARE, 1)
    fetched = []
    for k in (1, 2, 3):
        target_half = (y + NY - k) % NY // 2
        piece = lax.dynamic_index_in_dim(share, target_half, 0, keepdims=False)
        fetched.append(move(piece, 0, -k))
    fetched = jnp.concatenate(fetched)
    up1, down1 = move_x(fetched, -1), move_x(fetched, 1)
    up2, down2 = move_x(up1[:96], -1), move_x(down1[96:], 1)
    line = jnp.concatenate([fetched, up1, up2, down2, down1])
    other_line = swap_wa(line, 1)
    own_left = lax.dynamic_index_in_dim(left, half, 0, keepdims=False)

    right_own = lax.dynamic_slice_in_dim(noise_right, parity * 512, 512, 1)
    right_not = lax.dynamic_slice_in_dim(noise_right, (1 - parity) * 512, 512, 1)
    right_line = jnp.stack(
        [move(right_not, 0, -1), move(right_own, 0, -2), move(right_not, 0, 1)]
    )

    projected = jnp.sum(inputs.astype(f32) * noise_left.astype(f32), axis=1) / math.sqrt(D)
    outputs = (
        jnp.concatenate([out_first, out_second], axis=1)
        + noise_scale * projected[:, None] * noise_right.astype(f32)
    )
    reward = jnp.sum(jnp.tanh(outputs) * reward_probe[None, :], axis=1) / math.sqrt(F)
    reward = reward.reshape(4, 128)
    for mask in (1, 2, 4):
        reward = reward + swap_wa(reward, mask)
    raw = reward.reshape(MEMBERS) + scores.astype(f32) / 16.0

    raw_tile = raw.reshape(4, 128)
    raw_line = jnp.stack([move(raw_tile, 0, -k).reshape(MEMBERS) for k in (1, 2, 3)])
    sums = jnp.stack(
        [
            jnp.sum(raw) + jnp.sum(raw_line),
            jnp.sum(raw * raw) + jnp.sum(raw_line * raw_line),
        ]
    )
    for mask in (NY, 2 * NY, 4 * NY):
        sums = sums + swap_pop(sums, mask)
    center = sums[0] / population
    spread = sums[1] / population - center * center
    scale = lax.rsqrt(spread + epsilon)

    def scaled(values, right):
        fit = (values - center) * scale
        return ((fit / math.sqrt(population))[:, None] * right.astype(f32)).astype(bf16)

    fitness = (raw - center) * scale
    members = [
        (own_left, scaled(raw, right_own)),
        (line, scaled(line_order(raw_line, x, core), line_order(right_line, x, core))),
        (
            other_line,
            scaled(line_order(raw_line, x, 1 - core), line_order(right_line, x, 1 - core)),
        ),
    ]

    def part(dz):
        return sum(
            update_dot(rows[:, dz * 256 : (dz + 1) * 256], right) for rows, right in members
        )

    far = part(4)
    up = move(far[:, :256].astype(bf16), 1, 0)
    down = move(far[:, 256:].astype(bf16), -1, 0)
    none = jnp.zeros((256, 256), f32)
    up = jnp.concatenate([up.astype(f32), none], axis=1)
    down = jnp.concatenate([none, down.astype(f32)], axis=1)
    for distance in (3, 2, 1):
        up = move((part(distance) + up).astype(bf16), 1, 0).astype(f32)
        down = move((part(NZ - distance) + down).astype(bf16), -1, 0).astype(f32)
    rows = (part(0) + up + down).reshape(2, 128, 512)
    mine = lax.dynamic_index_in_dim(rows, parity, 0, keepdims=False)
    theirs = lax.dynamic_index_in_dim(rows, 1 - parity, 0, keepdims=False)
    received = swap_pop(theirs.astype(bf16), 1).astype(f32)
    update = jnp.where(
        parity == 0,
        jnp.concatenate([mine, received], axis=1),
        jnp.concatenate([received, mine], axis=1),
    )
    new_master = master + learn_rate * update
    return (fitness, update, new_master, new_master.astype(bf16))


def solution(mesh):
    return jax.shard_map(
        shards,
        mesh=mesh,
        in_specs=(
            P("pop", None),
            P("pop", None),
            P("pop", "wa"),
            P("wa"),
            P("pop"),
            P("pop", "wa"),
        ),
        out_specs=(P("pop"), P("pop", "wa"), P("pop", "wa"), P("pop", "wa")),
        check_vma=False,
    )
```

```python
import math

import jax
import jax.numpy as jnp
from jax import lax
from jax.experimental import pallas as pl
from jax.experimental.pallas import tpu as pltpu
from jax.sharding import PartitionSpec as P

D = 4096
F = 8192
NZ, NY, NX = 8, 4, 4
MEMBERS = 512
POPULATION = MEMBERS * NZ * NY
OTHERS = 3 * MEMBERS // 2
SHARE = 64

noise_scale = 0.5
learn_rate = 0.01
epsilon = 1e-05

bf16 = jnp.bfloat16
f32 = jnp.float32


def move(value, dz, dy):
    pairs = [
        (z * NY + y, (z + dz) % NZ * NY + (y + dy) % NY)
        for z in range(NZ)
        for y in range(NY)
    ]
    return lax.ppermute(value, "pop", pairs)


def swap_pop(value, mask):
    return lax.ppermute(value, "pop", [(i, i ^ mask) for i in range(NZ * NY)])


def swap_wa(value, mask):
    return lax.ppermute(value, "wa", [(i, i ^ mask) for i in range(2 * NX)])


def move_x(value, dx):
    pairs = [
        (2 * x + c, 2 * ((x + dx) % NX) + c) for x in range(NX) for c in range(2)
    ]
    return lax.ppermute(value, "wa", pairs)


def forward_kernel(pieces, has_total, last, place, inputs, line, other_line, *refs):
    refs = list(refs)
    pieces_in = [refs.pop(0) for _ in pieces]
    total_in = refs.pop(0) if has_total else None
    if last:
        projected, right, right_partner, probe = [refs.pop(0) for _ in range(4)]
    out = refs.pop(0)
    total = refs.pop(0) if last else out
    weights, gathered, arrived = refs
    z, x, core = place[0], place[1], place[2]
    copies, at = [], 0
    for index, ((dz, first, depth), piece) in enumerate(zip(pieces, pieces_in)):
        here = pl.ds(at, depth)
        columns = pl.ds(pl.multiple_of(lax.rem(z + dz, NZ) * 512 + first, 128), depth)
        moves = [
            (piece, weights.at[here, :]),
            (inputs.at[:, columns], gathered.at[pl.ds(0, MEMBERS), here]),
        ]
        for dx in range(NX):
            owner = 2 * lax.rem(x + dx, NX)
            for source, rest in ((line, core), (other_line, 1 - core)):
                row = pl.multiple_of(MEMBERS + (owner + rest) * SHARE, SHARE)
                moves.append(
                    (
                        source.at[pl.ds(dx * SHARE, SHARE), columns],
                        gathered.at[pl.ds(row, SHARE), here],
                    )
                )
        for number, (source, target) in enumerate(moves):
            copies.append(
                pltpu.make_async_copy(source, target, arrived.at[index * len(moves) + number])
            )
            copies[-1].start()
        at += depth
    at, each = 0, len(copies) // len(pieces)
    for index, (_, _, depth) in enumerate(pieces):
        for copy in copies[index * each : (index + 1) * each]:
            copy.wait()
        for row in range(0, 2 * MEMBERS, 256):
            rows = pl.ds(row, 256)
            term = jnp.dot(
                gathered[rows, at : at + depth],
                weights[at : at + depth, :],
                preferred_element_type=f32,
            )
            if index:
                term = term + total[rows, :]
            elif has_total:
                term = term + total_in[rows, :]
            total[rows, :] = term
        at += depth
    if last:
        for group in range(2 * MEMBERS // 128):
            own = group < MEMBERS // 128
            rows = pl.ds(group * 128, 128)
            noise = right if own else right_partner
            noise_rows = pl.ds(group % (MEMBERS // 128) * 128, 128)
            wide = noise_scale * jnp.transpose(
                jnp.broadcast_to(projected[group : group + 1, :], (128, 128))
            )
            terms = jnp.zeros((128, 128), f32)
            for lane in range(0, 512, 128):
                lanes = pl.ds(lane, 128)
                outputs = total[rows, lanes] + wide * noise[noise_rows, lanes].astype(f32)
                terms = terms + jnp.tanh(outputs) * probe[:, lanes]
            out[pl.ds(group, 1), :] = jnp.sum(
                jnp.transpose(terms), axis=0, keepdims=True
            ) / math.sqrt(F)


def forward(place, rows, pieces, total=None, tail=None):
    plan = tuple(piece[:3] for piece in pieces)
    depth = sum(piece[2] for piece in pieces)
    vmem, hbm = pl.BlockSpec(memory_space=pltpu.VMEM), pl.BlockSpec(memory_space=pl.ANY)
    near = ([] if total is None else [total]) + ([] if tail is None else tail)
    scratch = [] if tail is None else [pltpu.VMEM((2 * MEMBERS, 512), f32)]
    scratch += [
        pltpu.VMEM((depth, 512), bf16),
        pltpu.VMEM((2 * MEMBERS, depth), bf16),
        pltpu.SemaphoreType.DMA((len(pieces) * (2 + 2 * NX),)),
    ]
    return pl.pallas_call(
        lambda *refs: forward_kernel(plan, total is not None, tail is not None, *refs),
        in_specs=[pl.BlockSpec(memory_space=pltpu.SMEM)]
        + [hbm] * (3 + len(pieces))
        + [vmem] * len(near),
        out_specs=vmem,
        out_shape=jax.ShapeDtypeStruct((2 * MEMBERS, 512) if tail is None else (8, 128), f32),
        scratch_shapes=scratch,
        compiler_params=pltpu.CompilerParams(vmem_limit_bytes=60 * 2**20),
        cost_estimate=pl.CostEstimate(
            flops=2 * 2 * MEMBERS * depth * 512,
            bytes_accessed=depth * 2 * 1536 + 4 * 2**20,
            transcendentals=0,
        ),
    )(place, *rows, *[piece[3] for piece in pieces], *near)


def update_kernel(place, left, line, other_line, right, right_line, right_other, out):
    total = update_dot(left[...], right[...])
    total += update_dot(line[...], right_line[...])
    out[0] = total + update_dot(other_line[...], right_other[...])


def first_kernel(
    place, sums, left, line, other_line, raw, right, right_1, right_2, right_3, *outs
):
    up, down, fitness, scaled, scaled_line, scaled_other = outs
    x, core = place[1], place[2]

    def total_of(tile):
        return jnp.sum(jnp.sum(tile, axis=1, keepdims=True), axis=0, keepdims=True)

    center = total_of(sums[:4, :]) / POPULATION
    spread = total_of(sums[4:, :]) / POPULATION - center * center
    scale = lax.rsqrt(spread + epsilon)
    fitness[...] = (raw[:4, :] - center) * scale

    def wide(row):
        fit = (raw[row, :] - center) * scale / math.sqrt(POPULATION)
        return jnp.transpose(jnp.broadcast_to(fit, (128, 128)))

    def store(target, at, count, fit, values):
        for lane in range(0, 512, 128):
            lanes = pl.ds(lane, 128)
            target[pl.ds(at, count), lanes] = (
                fit * values[:, lane : lane + 128].astype(f32)
            ).astype(bf16)

    for row in range(4):
        store(scaled, row * 128, 128, wide(pl.ds(row, 1)), right[pl.ds(row * 128, 128), :])
    at = 0
    for dx in range(NX):
        owner = lax.rem(x + dx, NX)
        for index, values in enumerate((right_1, right_2, right_3)):
            fit = wide(pl.ds(4 * index + 4 + owner, 1))
            low, high = fit[:SHARE], fit[SHARE:]
            for target, side in ((scaled_line, core), (scaled_other, 1 - core)):
                row = pl.multiple_of((2 * owner + side) * SHARE, SHARE)
                store(
                    target,
                    at,
                    SHARE,
                    jnp.where(side == 0, low, high),
                    values[pl.ds(row, SHARE), :],
                )
            at += SHARE
    total = update_dot(left[...], scaled[...])
    total += update_dot(line[...], scaled_line[...])
    total += update_dot(other_line[...], scaled_other[...])
    up[...] = total[:, :256].astype(bf16)
    down[...] = total[:, 256:].astype(bf16)


def left_specs(distance):
    return [
        pl.BlockSpec(
            (MEMBERS, 256),
            lambda i, s: (0, lax.rem(s[0] + distance(i), NZ) * 2 + s[3]),
        )
    ] + [
        pl.BlockSpec((OTHERS, 256), lambda i, s: (0, lax.rem(s[0] + distance(i), NZ)))
    ] * 2


def whole(shape, space=pltpu.VMEM):
    return pl.BlockSpec(shape, lambda i, s: (0,) * len(shape), memory_space=space)


def update_first(place, sums, left, line, other_line, raw, rights):
    shapes = [(MEMBERS, 512), (OTHERS, 512), (OTHERS, 512)]
    return pl.pallas_call(
        first_kernel,
        grid_spec=pltpu.PrefetchScalarGridSpec(
            num_scalar_prefetch=1,
            grid=(1,),
            in_specs=[whole((8, 128))]
            + left_specs(lambda i: 4)
            + [whole((16, 128))]
            + [whole((MEMBERS, 512))] * 4,
            out_specs=[whole((256, 256))] * 2
            + [whole((4, 128))]
            + [whole(shape) for shape in shapes],
        ),
        out_shape=[jax.ShapeDtypeStruct((256, 256), bf16)] * 2
        + [jax.ShapeDtypeStruct((4, 128), f32)]
        + [jax.ShapeDtypeStruct(shape, bf16) for shape in shapes],
        compiler_params=pltpu.CompilerParams(vmem_limit_bytes=40 * 2**20),
        cost_estimate=pl.CostEstimate(
            flops=2 * 2048 * 256 * 512, bytes_accessed=6 * 2**20, transcendentals=0
        ),
    )(place, sums, left, line, other_line, raw, *rights)


def update_rest(place, left, line, other_line, right, right_line, right_other, count, distance):
    return pl.pallas_call(
        update_kernel,
        grid_spec=pltpu.PrefetchScalarGridSpec(
            num_scalar_prefetch=1,
            grid=(count,),
            in_specs=left_specs(distance)
            + [whole((MEMBERS, 512)), whole((OTHERS, 512)), whole((OTHERS, 512))],
            out_specs=pl.BlockSpec((1, 256, 512), lambda i, s: (i, 0, 0)),
        ),
        out_shape=jax.ShapeDtypeStruct((count, 256, 512), f32),
        compiler_params=pltpu.CompilerParams(vmem_limit_bytes=40 * 2**20),
        cost_estimate=pl.CostEstimate(
            flops=2 * 2048 * 256 * 512, bytes_accessed=2**20, transcendentals=0
        ),
    )(place, left, line, other_line, right, right_line, right_other)


def update_dot(left, right):
    return lax.dot_general(
        left, right, (((0,), (0,)), ((), ())), preferred_element_type=f32
    )


def after(value, *others):
    return lax.optimization_barrier((value, *others))[0]


def shards(inputs, noise_left, noise_right, reward_probe, scores, master):
    pop, wa = lax.axis_index("pop"), lax.axis_index("wa")
    z, y = pop // NY, pop % NY
    x, core = wa // 2, wa % 2
    half, parity = y // 2, y % 2
    place = jnp.stack([z, x, core, half]).astype(jnp.int32)

    def halves(value):
        return (
            lax.dynamic_slice_in_dim(value, parity * 512, 512, 1),
            lax.dynamic_slice_in_dim(value, (1 - parity) * 512, 512, 1),
        )

    weight_own, weight_not = halves(master.astype(bf16))
    rel = [
        weight_own,
        swap_pop(weight_not, 1),
        swap_pop(weight_own, 2),
        swap_pop(weight_not, 3),
    ]
    odd, high = parity == 1, half == 1
    rel = [jnp.where(odd, rel[i ^ 1], rel[i]) for i in range(NY)]
    whole_y = jnp.concatenate([jnp.where(high, rel[i ^ 2], rel[i]) for i in range(NY)])

    share = lax.dynamic_slice_in_dim(inputs, wa * SHARE, SHARE, 0)
    share = swap_pop(share, 1)
    up1, down1 = move(whole_y, -1, 0), move(whole_y, 1, 0)
    share = after(share, whole_y)
    inputs_line = jnp.concatenate(
        [share, move_x(share, -1), move_x(share, 2), move_x(share, 1)]
    )

    projected = jnp.sum(inputs.astype(f32) * noise_left.astype(f32), axis=1) / math.sqrt(D)
    projected = projected.reshape(4, 128)
    share = lax.dynamic_slice_in_dim(noise_left, wa * SHARE, SHARE, 0)
    share = jnp.swapaxes(share.reshape(SHARE, NZ, 2, 256), 0, 2).swapaxes(1, 2)
    share = share.reshape(2, SHARE, D // 2)
    share_own = lax.dynamic_index_in_dim(share, half, 0, keepdims=False)
    share_not = lax.dynamic_index_in_dim(share, 1 - half, 0, keepdims=False)
    right_own, right_not = halves(noise_right)

    up2, down2 = move(up1, -1, 0), move(down1, 1, 0)
    inputs_other = swap_wa(after(inputs_line, up1, down1), 1)
    left_1 = swap_pop(after(share_own, up1, down1, inputs_line), 1)
    left_2 = swap_pop(after(share_not, up1, down1, inputs_line), 2)
    rows = (inputs, inputs_line, inputs_other)

    up3, down3 = move(up2, -1, 0), move(down2, 1, 0)
    left_3 = swap_pop(after(share_not, up2, down2, left_1, left_2), 3)
    right_1 = swap_pop(after(right_not, up2, down2, left_1), 1)
    right_3 = swap_pop(after(right_not, up2, down2, left_2), 3)
    total = forward(
        place, rows, [(0, 0, 512, whole_y), (1, 0, 512, up1), (7, 0, 512, down1)]
    )

    up4, down4 = move(up3[:256], -1, 0), move(down3[256:], 1, 0)
    fetched = after(jnp.concatenate([left_1, left_2, left_3]), up3, down3, right_1, total)
    line_1, line_3 = move_x(fetched, -1), move_x(fetched, 1)
    projected = jnp.concatenate([projected, swap_pop(after(projected, right_1), 1)])
    right_2 = swap_pop(after(right_own, up3, down3, right_3), 2)
    total = forward(
        place,
        rows,
        [(2, 0, 512, up2), (6, 0, 512, down2), (3, 0, 512, up3), (5, 0, 512, down3)],
        total,
    )
    probe = lax.dynamic_slice_in_dim(reward_probe, parity * 512, 512, 0).reshape(1, 512)
    reward = forward(
        place,
        rows,
        [(4, 0, 256, up4), (4, 256, 256, down4)],
        total,
        [projected, right_own, right_1, probe],
    )
    line_2 = move_x(after(fetched, line_1, line_3, total), 2)
    line = jnp.concatenate([fetched, line_1, line_2, line_3])
    other_line = swap_wa(line, 1)

    for mask in (1, 2, 4):
        reward = reward + swap_wa(reward, mask)
    own = reward[:4] + scores.astype(f32).reshape(4, 128) / 16.0
    reward = jnp.concatenate([own, reward[4:]])
    others = [swap_pop(reward, mask) for mask in (1, 2, 3)]
    raw = [
        own + others[0][4:],
        reward[4:] + others[0][:4],
        others[1][:4] + others[2][4:],
        others[1][4:] + others[2][:4],
    ]
    sums = jnp.concatenate(
        [raw[0] + raw[1] + raw[2] + raw[3], sum(tile * tile for tile in raw)]
    )
    for mask in (NY, 2 * NY, 4 * NY):
        sums = sums + swap_pop(sums, mask)

    up, down, fitness, *scaled = update_first(
        place,
        sums,
        noise_left,
        line,
        other_line,
        jnp.concatenate(raw),
        (right_own, right_1, right_2, right_3),
    )
    members = (place, noise_left, line, other_line, *scaled)
    next_parts = update_rest(*members, 2, lambda i: 3 + 2 * i)
    up = move(up, 1, 0).astype(f32)
    down = move(down, -1, 0).astype(f32)
    none = jnp.zeros((256, 256), f32)
    up = jnp.concatenate([up, none], axis=1)
    down = jnp.concatenate([none, down], axis=1)
    parts = update_rest(
        *members,
        5,
        lambda i: jnp.where(i == 4, 0, jnp.where(lax.rem(i, 2) == 0, 2 - i // 2, 6 + i // 2)),
    )
    for up_part, down_part in (
        (next_parts[0], next_parts[1]),
        (parts[0], parts[1]),
        (parts[2], parts[3]),
    ):
        up = move((up_part + up).astype(bf16), 1, 0).astype(f32)
        down = move((down_part + down).astype(bf16), -1, 0).astype(f32)
    rows = (parts[4] + up + down).reshape(2, 128, 512)
    mine = lax.dynamic_index_in_dim(rows, parity, 0, keepdims=False)
    theirs = lax.dynamic_index_in_dim(rows, 1 - parity, 0, keepdims=False)
    received = swap_pop(theirs.astype(bf16), 1).astype(f32)
    update = jnp.where(
        parity == 0,
        jnp.concatenate([mine, received], axis=1),
        jnp.concatenate([received, mine], axis=1),
    )
    new_master = master + learn_rate * update
    return (fitness.reshape(MEMBERS), update, new_master, new_master.astype(bf16))


def solution(mesh):
    return jax.shard_map(
        shards,
        mesh=mesh,
        in_specs=(
            P("pop", None),
            P("pop", None),
            P("pop", "wa"),
            P("wa"),
            P("pop"),
            P("pop", "wa"),
        ),
        out_specs=(P("pop"), P("pop", "wa"), P("pop", "wa"), P("pop", "wa")),
        check_vma=False,
    )
```

```python
import math

import jax
import jax.numpy as jnp
from jax import lax
from jax.experimental import pallas as pl
from jax.experimental.pallas import tpu as pltpu
from jax.sharding import PartitionSpec as P

D = 4096
F = 8192
NZ, NY, NX = 8, 4, 4
MEMBERS = 512
POPULATION = MEMBERS * NZ * NY
OTHERS = 3 * MEMBERS
SHARE = 64

noise_scale = 0.5
learn_rate = 0.01
epsilon = 1e-05

bf16 = jnp.bfloat16
f32 = jnp.float32


def move(value, dz, dy):
    pairs = [
        (z * NY + y, (z + dz) % NZ * NY + (y + dy) % NY)
        for z in range(NZ)
        for y in range(NY)
    ]
    return lax.ppermute(value, "pop", pairs)


def swap_pop(value, mask):
    return lax.ppermute(value, "pop", [(i, i ^ mask) for i in range(NZ * NY)])


def swap_wa(value, mask):
    return lax.ppermute(value, "wa", [(i, i ^ mask) for i in range(2 * NX)])


def after(value, *others):
    return lax.optimization_barrier((value, *others))[0]


def load_pieces(z, plan, sources, pieces, gathered, weights, arrived):
    copies, at = [], 0
    for (dz, depth), piece in zip(plan, pieces):
        here = pl.ds(at, depth)
        columns = pl.ds(pl.multiple_of(lax.rem(z + dz, NZ) * 512, 512), depth)
        moves = [(piece, weights.at[here, :])]
        for index, source in enumerate(sources):
            rows = pl.ds(index * MEMBERS, MEMBERS)
            moves.append((source.at[:, columns], gathered.at[rows, here]))
        for source, target in moves:
            copies.append(pltpu.make_async_copy(source, target, arrived.at[len(copies)]))
            copies[-1].start()
        at += depth
    return copies


def forward_kernel(plan, has_total, place, source, *refs):
    pieces = refs[: len(plan)]
    total_in = refs[len(plan)] if has_total else None
    out, weights, gathered, arrived = refs[-4:]
    copies = load_pieces(place[0], plan, [source], pieces, gathered, weights, arrived)
    cut = len(plan) // 2 if len(plan) > 4 else len(plan)
    for first, last in ((0, cut), (cut, len(plan))):
        if first == last:
            continue
        for copy in copies[2 * first : 2 * last]:
            copy.wait()
        for row in range(0, MEMBERS, 256):
            rows = pl.ds(row, 256)
            term = jnp.dot(
                gathered[rows, first * 512 : last * 512],
                weights[first * 512 : last * 512, :],
                preferred_element_type=f32,
            )
            if first:
                term = term + out[rows, :]
            elif has_total:
                term = term + total_in[rows, :]
            out[rows, :] = term


def forward(place, source, pieces, total=None):
    plan = tuple((dz, 512) for dz, _ in pieces)
    depth = 512 * len(plan)
    vmem, hbm = pl.BlockSpec(memory_space=pltpu.VMEM), pl.BlockSpec(memory_space=pl.ANY)
    totals = [] if total is None else [total]
    return pl.pallas_call(
        lambda *refs: forward_kernel(plan, total is not None, *refs),
        in_specs=[pl.BlockSpec(memory_space=pltpu.SMEM)]
        + [hbm] * (1 + len(pieces))
        + [vmem] * len(totals),
        out_specs=vmem,
        out_shape=jax.ShapeDtypeStruct((MEMBERS, 512), f32),
        scratch_shapes=[
            pltpu.VMEM((depth, 512), bf16),
            pltpu.VMEM((MEMBERS, depth), bf16),
            pltpu.SemaphoreType.DMA((2 * len(plan),)),
        ],
        compiler_params=pltpu.CompilerParams(vmem_limit_bytes=60 * 2**20),
        cost_estimate=pl.CostEstimate(
            flops=2 * MEMBERS * depth * 512,
            bytes_accessed=depth * 2 * 1024 + 2 * 2**20,
            transcendentals=0,
        ),
    )(place, source, *[piece for _, piece in pieces], *totals)


def reward_kernel(plan, place, inputs, partner, *refs):
    pieces, refs = refs[: len(plan)], refs[len(plan) :]
    own, other, projected, right, right_1, probe, out, weights, gathered, arrived = refs
    copies = load_pieces(
        place[0], plan, [inputs, partner], pieces, gathered, weights, arrived
    )
    first = pl.multiple_of(place[1] * 512, 512)
    for copy in copies:
        copy.wait()
    for group in range(2 * MEMBERS // 128):
        mine = group < MEMBERS // 128
        total, noise = (own, right) if mine else (other, right_1)
        rows = pl.ds(group % (MEMBERS // 128) * 128, 128)
        outputs = total[rows, :] + jnp.dot(
            gathered[group * 128 : (group + 1) * 128, :],
            weights[...],
            preferred_element_type=f32,
        )
        wide = noise_scale * jnp.transpose(
            jnp.broadcast_to(projected[group : group + 1, :], (128, 128))
        )
        terms = jnp.zeros((128, 128), f32)
        for lane in range(0, 512, 128):
            drawn = noise[rows, pl.ds(pl.multiple_of(first + lane, 128), 128)].astype(f32)
            lanes = outputs[:, lane : lane + 128] + wide * drawn
            terms = terms + jnp.tanh(lanes) * probe[:, lane : lane + 128]
        out[pl.ds(group, 1), :] = jnp.sum(
            jnp.transpose(terms), axis=0, keepdims=True
        ) / math.sqrt(F)


def reward_terms(place, inputs, partner, pieces, *operands):
    plan = tuple((dz, 512) for dz, _ in pieces)
    depth = 512 * len(plan)
    vmem, hbm = pl.BlockSpec(memory_space=pltpu.VMEM), pl.BlockSpec(memory_space=pl.ANY)
    return pl.pallas_call(
        lambda *refs: reward_kernel(plan, *refs),
        in_specs=[pl.BlockSpec(memory_space=pltpu.SMEM)]
        + [hbm] * (2 + len(plan))
        + [vmem] * len(operands),
        out_specs=vmem,
        out_shape=jax.ShapeDtypeStruct((8, 128), f32),
        scratch_shapes=[
            pltpu.VMEM((depth, 512), bf16),
            pltpu.VMEM((2 * MEMBERS, depth), bf16),
            pltpu.SemaphoreType.DMA((3 * len(plan),)),
        ],
        compiler_params=pltpu.CompilerParams(vmem_limit_bytes=60 * 2**20),
        cost_estimate=pl.CostEstimate(
            flops=4 * MEMBERS * depth * 512, bytes_accessed=6 * 2**20, transcendentals=0
        ),
    )(place, inputs, partner, *[piece for _, piece in pieces], *operands)


def update_dot(left, right):
    return lax.dot_general(
        left, right, (((0,), (0,)), ((), ())), preferred_element_type=f32
    )


def plane_sum(count, lefts, lines, right, right_line):
    left = jnp.concatenate([ref[...] for ref in lefts], axis=1)
    line = jnp.concatenate([ref[...] for ref in lines], axis=1)
    return update_dot(left, right[...]) + update_dot(line, right_line[...])


def update_kernel(count, place, *refs):
    lefts, lines = refs[:count], refs[count : 2 * count]
    right, right_line, out = refs[2 * count :]
    total = plane_sum(count, lefts, lines, right, right_line)
    for index in range(count):
        out[index] = total[index * 128 : (index + 1) * 128]


def first_kernel(place, sums, left, line, raw, right, right_1, right_2, right_3, *outs):
    up, down, fitness, scaled, scaled_line = outs

    def total_of(tile):
        return jnp.sum(jnp.sum(tile, axis=1, keepdims=True), axis=0, keepdims=True)

    center = total_of(sums[:4, :]) / POPULATION
    spread = total_of(sums[4:, :]) / POPULATION - center * center
    scale = lax.rsqrt(spread + epsilon)
    fitness[...] = (raw[:4, :] - center) * scale

    def wide(row):
        fit = (raw[row : row + 1, :] - center) * scale / math.sqrt(POPULATION)
        return jnp.transpose(jnp.broadcast_to(fit, (128, 128)))

    def store(target, at, fit, values, row):
        count = fit.shape[0]
        for lane in range(0, 1024, 128):
            drawn = values[row : row + count, lane : lane + 128].astype(f32)
            target[at : at + count, lane : lane + 128] = (fit * drawn).astype(bf16)

    for row in range(4):
        store(scaled, row * 128, wide(row), right, row * 128)
    for index, values in enumerate((right_1, right_2, right_3)):
        for row in range(4):
            fit = wide(4 * index + 4 + row)
            for side in range(2):
                owner = 2 * row + side
                part = fit[side * SHARE : (side + 1) * SHARE]
                store(scaled_line, (3 * owner + index) * SHARE, part, values, owner * SHARE)
    total = plane_sum(1, [left], [line], scaled, scaled_line)
    up[...] = total[:, :512].astype(bf16)
    down[...] = total[:, 512:].astype(bf16)


def left_specs(distances):
    def of(rows, turn):
        return [
            pl.BlockSpec((rows, 128), lambda i, s, dz=dz: (0, turn(lax.rem(s[0] + dz, NZ), s)))
            for dz in distances
        ]

    return of(MEMBERS, lambda z, s: z * NY + s[2]) + of(OTHERS, lambda z, s: z)


def whole(shape):
    return pl.BlockSpec(shape, lambda i, s: (0,) * len(shape))


def update_first(place, sums, left, line, raw, rights):
    shapes = [(MEMBERS, 1024), (OTHERS, 1024)]
    return pl.pallas_call(
        first_kernel,
        grid_spec=pltpu.PrefetchScalarGridSpec(
            num_scalar_prefetch=1,
            grid=(1,),
            in_specs=[whole((8, 128))]
            + left_specs((4,))
            + [whole((16, 128))]
            + [whole((MEMBERS, 1024))] * 4,
            out_specs=[whole((128, 512))] * 2
            + [whole((4, 128))]
            + [whole(shape) for shape in shapes],
        ),
        out_shape=[jax.ShapeDtypeStruct((128, 512), bf16)] * 2
        + [jax.ShapeDtypeStruct((4, 128), f32)]
        + [jax.ShapeDtypeStruct(shape, bf16) for shape in shapes],
        compiler_params=pltpu.CompilerParams(vmem_limit_bytes=40 * 2**20),
        cost_estimate=pl.CostEstimate(
            flops=2 * 2048 * 256 * 512, bytes_accessed=6 * 2**20, transcendentals=0
        ),
    )(place, sums, left, line, raw, *rights)


def update_rest(place, left, line, right, right_line, distances):
    count = len(distances)
    return pl.pallas_call(
        lambda *refs: update_kernel(count, *refs),
        grid_spec=pltpu.PrefetchScalarGridSpec(
            num_scalar_prefetch=1,
            grid=(1,),
            in_specs=left_specs(distances) + [whole((MEMBERS, 1024)), whole((OTHERS, 1024))],
            out_specs=pl.BlockSpec((count, 128, 1024), lambda i, s: (0, 0, 0)),
        ),
        out_shape=jax.ShapeDtypeStruct((count, 128, 1024), f32),
        compiler_params=pltpu.CompilerParams(vmem_limit_bytes=40 * 2**20),
        cost_estimate=pl.CostEstimate(
            flops=2 * 2048 * 256 * 512, bytes_accessed=2**20, transcendentals=0
        ),
    )(place, *[left] * count, *[line] * count, right, right_line)


def shards(inputs, noise_left, noise_right, reward_probe, scores, master):
    pop, wa = lax.axis_index("pop"), lax.axis_index("wa")
    z, y = pop // NY, pop % NY
    half, parity = y // 2, y % 2
    place = jnp.stack([z, parity, y]).astype(jnp.int32)

    weight = master.astype(bf16)
    weight_own = lax.dynamic_slice_in_dim(weight, parity * 512, 512, 1)
    weight_not = lax.dynamic_slice_in_dim(weight, (1 - parity) * 512, 512, 1)
    rel = [
        weight_own,
        swap_pop(weight_not, 1),
        swap_pop(weight_own, 2),
        swap_pop(weight_not, 3),
    ]
    odd, high = parity == 1, half == 1
    rel = [jnp.where(odd, rel[i ^ 1], rel[i]) for i in range(NY)]
    whole_y = jnp.concatenate([jnp.where(high, rel[i ^ 2], rel[i]) for i in range(NY)])

    up1, down1 = move(whole_y, -1, 0), move(whole_y, 1, 0)
    share = lax.dynamic_slice_in_dim(inputs, wa * SHARE, SHARE, 0)
    share = swap_pop(after(share, whole_y), 1)
    partner = lax.all_gather(after(share, up1, down1), "wa", axis=0, tiled=True)
    left_share = lax.dynamic_slice_in_dim(noise_left, wa * SHARE, SHARE, 0)
    left_share = jnp.swapaxes(left_share.reshape(SHARE, NZ, NY, 128), 0, 2).swapaxes(1, 2)
    left_share = left_share.reshape(NY, SHARE, D // NY)
    left_share = [
        lax.dynamic_index_in_dim(left_share, y ^ mask, 0, keepdims=False) for mask in (1, 2, 3)
    ]
    projected = jnp.sum(inputs.astype(f32) * noise_left.astype(f32), axis=1) / math.sqrt(D)
    projected = projected.reshape(4, 128)
    right_3 = swap_pop(after(noise_right, whole_y, projected), 3)

    up1, down1 = lax.optimization_barrier((up1, down1))
    up2, down2 = move(up1, -1, 0), move(down1, 1, 0)
    projected = jnp.concatenate([projected, swap_pop(after(projected, up1), 1)])
    right_1 = swap_pop(after(noise_right, up1, projected), 1)
    total = forward(place, inputs, [(0, whole_y), (1, up1), (7, down1)])

    up2, down2, right_3, projected = lax.optimization_barrier(
        (up2, down2, right_3, projected)
    )
    up3, down3 = move(up2, -1, 0), move(down2, 1, 0)
    total = forward(place, inputs, [(2, up2), (6, down2)], total)

    up3, down3, total, right_1 = lax.optimization_barrier((up3, down3, total, right_1))
    far = move(up3, -1, 0)
    fetched = jnp.concatenate(
        [swap_pop(after(left_share[mask - 1], up3), mask) for mask in (1, 2, 3)]
    )
    right_2 = swap_pop(after(noise_right, up3), 2)
    other = forward(
        place, partner, [(0, whole_y), (1, up1), (7, down1), (2, up2), (6, down2)]
    )
    line = lax.all_gather(after(fetched, partner, far), "wa", axis=0, tiled=True)
    probe = lax.dynamic_slice_in_dim(reward_probe, parity * 512, 512, 0).reshape(1, 512)
    reward = reward_terms(
        place,
        inputs,
        partner,
        [(3, up3), (5, down3), (4, far)],
        total,
        other,
        projected,
        noise_right,
        right_1,
        probe,
    )

    reward = reward + swap_wa(reward, 1)
    pair = [swap_wa(reward, mask) for mask in (2, 4, 6)]
    reward = after((reward + pair[0]) + (pair[1] + pair[2]), right_2)
    own = reward[:4] + scores.astype(f32).reshape(4, 128) / 16.0
    reward = jnp.concatenate([own, reward[4:]])
    others = [swap_pop(reward, mask) for mask in (1, 2, 3)]
    raw = [
        own + others[0][4:],
        reward[4:] + others[0][:4],
        others[1][:4] + others[2][4:],
        others[1][4:] + others[2][:4],
    ]
    sums = jnp.concatenate(
        [raw[0] + raw[1] + raw[2] + raw[3], sum(tile * tile for tile in raw)]
    )
    sums = sums + move(sums, 1, 0) + move(sums, -1, 0) + move(sums, 2, 0)
    sums = sums + move(sums, 4, 0)

    up, down, fitness, *scaled = update_first(
        place,
        sums,
        noise_left,
        line,
        jnp.concatenate(raw),
        (noise_right, right_1, right_2, right_3),
    )
    up = move(up, 1, 0).astype(f32)
    down = move(down, -1, 0).astype(f32)
    none = jnp.zeros((128, 512), f32)
    up = jnp.concatenate([up, none], axis=1)
    down = jnp.concatenate([none, down], axis=1)
    for distances in ((3, 5), (2, 6), (1, 7, 0)):
        parts = update_rest(place, noise_left, line, *scaled, distances)
        up = move((parts[0] + up).astype(bf16), 1, 0).astype(f32)
        down = move((parts[1] + down).astype(bf16), -1, 0).astype(f32)
    update = parts[2] + up + down
    new_master = master + learn_rate * update
    return (fitness.reshape(MEMBERS), update, new_master, new_master.astype(bf16))


def solution(mesh):
    return jax.shard_map(
        shards,
        mesh=mesh,
        in_specs=(
            P("pop", None),
            P("pop", None),
            P("pop", "wa"),
            P("wa"),
            P("pop"),
            P("pop", "wa"),
        ),
        out_specs=(P("pop"), P("pop", "wa"), P("pop", "wa"), P("pop", "wa")),
        check_vma=False,
    )
```

```python
import math

import jax
import jax.numpy as jnp
from jax import lax
from jax.experimental import pallas as pl
from jax.experimental.pallas import tpu as pltpu
from jax.sharding import PartitionSpec as P

D = 4096
F = 8192
NZ, NY, NX = 8, 4, 4
MEMBERS = 512
POPULATION = MEMBERS * NZ * NY
OTHERS = 3 * MEMBERS
SHARE = 64

noise_scale = 0.5
learn_rate = 0.01
epsilon = 1e-05

bf16 = jnp.bfloat16
f32 = jnp.float32


def move(value, dz, dy):
    pairs = [
        (z * NY + y, (z + dz) % NZ * NY + (y + dy) % NY)
        for z in range(NZ)
        for y in range(NY)
    ]
    return lax.ppermute(value, "pop", pairs)


def swap_pop(value, mask):
    return lax.ppermute(value, "pop", [(i, i ^ mask) for i in range(NZ * NY)])


def swap_wa(value, mask):
    return lax.ppermute(value, "wa", [(i, i ^ mask) for i in range(2 * NX)])


def after(value, *others):
    return lax.optimization_barrier((value, *others))[0]


def load_pieces(place, plan, own, parts, pieces, gathered, weights, arrived):
    copies, at = [], 0
    for (dz, depth), piece in zip(plan, pieces):
        here = pl.ds(at, depth)
        columns = pl.ds(pl.multiple_of(lax.rem(place[0] + dz, NZ) * 512, 512), depth)
        moves = [(piece, weights.at[here, :])]
        for source in own:
            moves.append((source.at[:, columns], gathered.at[pl.ds(0, MEMBERS), here]))
        for index, part in enumerate(parts):
            row = len(own) * MEMBERS + pl.multiple_of((place[3] ^ index) * SHARE, SHARE)
            moves.append((part.at[:, columns], gathered.at[pl.ds(row, SHARE), here]))
        for source, target in moves:
            copies.append(pltpu.make_async_copy(source, target, arrived.at[len(copies)]))
            copies[-1].start()
        at += depth
    return copies


def forward_kernel(plan, counts, place, *refs):
    refs = list(refs)
    own, parts, pieces, totals = [[refs.pop(0) for _ in range(count)] for count in counts]
    out, weights, gathered, arrived = refs
    copies = load_pieces(place, plan, own, parts, pieces, gathered, weights, arrived)
    for copy in copies:
        copy.wait()
    term = jnp.dot(gathered[...], weights[...], preferred_element_type=f32)
    for total in totals:
        term = term + total[...]
    out[...] = term


def forward(place, own, parts, pieces, totals=()):
    plan = tuple((dz, 512) for dz, _ in pieces)
    depth = 512 * len(plan)
    vmem, hbm = pl.BlockSpec(memory_space=pltpu.VMEM), pl.BlockSpec(memory_space=pl.ANY)
    counts = (len(own), len(parts), len(pieces), len(totals))
    return pl.pallas_call(
        lambda *refs: forward_kernel(plan, counts, *refs),
        in_specs=[pl.BlockSpec(memory_space=pltpu.SMEM)]
        + [hbm] * sum(counts[:3])
        + [vmem] * len(totals),
        out_specs=vmem,
        out_shape=jax.ShapeDtypeStruct((MEMBERS, 512), f32),
        scratch_shapes=[
            pltpu.VMEM((depth, 512), bf16),
            pltpu.VMEM((MEMBERS, depth), bf16),
            pltpu.SemaphoreType.DMA(((1 + len(own) + len(parts)) * len(plan),)),
        ],
        compiler_params=pltpu.CompilerParams(vmem_limit_bytes=60 * 2**20),
        cost_estimate=pl.CostEstimate(
            flops=2**20, bytes_accessed=2**16, transcendentals=0
        ),
    )(place, *own, *parts, *[piece for _, piece in pieces], *totals)


def both_kernel(plan, tail, place, inputs, *refs):
    parts, pieces, refs = refs[:8], refs[8 : 8 + len(plan)], refs[8 + len(plan) :]
    total, out_own, out_other, weights, gathered, gathered_own, arrived, arrived_own = refs
    copies = load_pieces(place, plan, [], parts, pieces, gathered, weights, arrived)
    for index, (dz, depth) in enumerate(tail):
        columns = pl.ds(pl.multiple_of(lax.rem(place[0] + dz, NZ) * 512, 512), depth)
        copies.append(
            pltpu.make_async_copy(
                inputs.at[:, columns],
                gathered_own.at[:, pl.ds(index * 512, 512)],
                arrived_own.at[index],
            )
        )
        copies[-1].start()
    for copy in copies:
        copy.wait()
    out_other[...] = jnp.dot(gathered[...], weights[...], preferred_element_type=f32)
    out_own[...] = total[...] + jnp.dot(
        gathered_own[...],
        weights[512 * (len(plan) - len(tail)) :, :],
        preferred_element_type=f32,
    )


def forward_both(place, inputs, parts, pieces, tail, total):
    plan = tuple((dz, 512) for dz, _ in pieces)
    depth = 512 * len(plan)
    vmem, hbm = pl.BlockSpec(memory_space=pltpu.VMEM), pl.BlockSpec(memory_space=pl.ANY)
    return pl.pallas_call(
        lambda *refs: both_kernel(plan, plan[-tail:], *refs),
        in_specs=[pl.BlockSpec(memory_space=pltpu.SMEM)]
        + [hbm] * (9 + len(pieces))
        + [vmem],
        out_specs=[vmem, vmem],
        out_shape=[jax.ShapeDtypeStruct((MEMBERS, 512), f32)] * 2,
        scratch_shapes=[
            pltpu.VMEM((depth, 512), bf16),
            pltpu.VMEM((MEMBERS, depth), bf16),
            pltpu.VMEM((MEMBERS, 512 * tail), bf16),
            pltpu.SemaphoreType.DMA((9 * len(plan),)),
            pltpu.SemaphoreType.DMA((tail,)),
        ],
        compiler_params=pltpu.CompilerParams(vmem_limit_bytes=60 * 2**20),
        cost_estimate=pl.CostEstimate(
            flops=2 * MEMBERS * depth * 512, bytes_accessed=8 * 2**20, transcendentals=0
        ),
    )(place, inputs, *parts, *[piece for _, piece in pieces], total)


def reward_kernel(plan, place, inputs, *refs):
    parts, pieces, refs = refs[:8], refs[8 : 8 + len(plan)], refs[8 + len(plan) :]
    own, other, projected, right, right_1, probe, out, weights, gathered, added, arrived = refs
    copies = load_pieces(
        place, plan, [inputs], parts, pieces, gathered, weights, arrived
    )
    first = pl.multiple_of(place[1] * 512, 512)
    for copy in copies:
        copy.wait()
    for group in range(2 * MEMBERS // 128):
        mine = group < MEMBERS // 128
        total, noise = (own, right) if mine else (other, right_1)
        row = group % (MEMBERS // 128) * 128
        rows = pl.ds(row, 128)
        if row == 0:
            added[...] = jnp.dot(
                gathered[group * 128 : group * 128 + MEMBERS, :],
                weights[...],
                preferred_element_type=f32,
            )
        outputs = total[rows, :] + added[rows, :]
        wide = noise_scale * jnp.transpose(
            jnp.broadcast_to(projected[group : group + 1, :], (128, 128))
        )
        terms = jnp.zeros((128, 128), f32)
        for lane in range(0, 512, 128):
            drawn = noise[rows, pl.ds(pl.multiple_of(first + lane, 128), 128)].astype(f32)
            lanes = outputs[:, lane : lane + 128] + wide * drawn
            terms = terms + jnp.tanh(lanes) * probe[:, lane : lane + 128]
        out[pl.ds(group, 1), :] = jnp.sum(
            jnp.transpose(terms), axis=0, keepdims=True
        ) / math.sqrt(F)


def reward_terms(place, inputs, parts, pieces, *operands):
    plan = tuple((dz, 512) for dz, _ in pieces)
    depth = 512 * len(plan)
    vmem, hbm = pl.BlockSpec(memory_space=pltpu.VMEM), pl.BlockSpec(memory_space=pl.ANY)
    return pl.pallas_call(
        lambda *refs: reward_kernel(plan, *refs),
        in_specs=[pl.BlockSpec(memory_space=pltpu.SMEM)]
        + [hbm] * (9 + len(plan))
        + [vmem] * len(operands),
        out_specs=vmem,
        out_shape=jax.ShapeDtypeStruct((8, 128), f32),
        scratch_shapes=[
            pltpu.VMEM((depth, 512), bf16),
            pltpu.VMEM((2 * MEMBERS, depth), bf16),
            pltpu.VMEM((MEMBERS, 512), f32),
            pltpu.SemaphoreType.DMA((10 * len(plan),)),
        ],
        compiler_params=pltpu.CompilerParams(vmem_limit_bytes=60 * 2**20),
        cost_estimate=pl.CostEstimate(
            flops=4 * MEMBERS * depth * 512, bytes_accessed=6 * 2**20, transcendentals=0
        ),
    )(place, inputs, *parts, *[piece for _, piece in pieces], *operands)


def line_kernel(place, *refs):
    parts, out, arrived = refs[:2], refs[2], refs[3]
    copies = []
    for index in range(2 * NX):
        for other in range(3):
            row = pl.multiple_of((3 * (place[3] ^ index) + other) * SHARE, SHARE)
            copies.append(
                pltpu.make_async_copy(
                    parts[index % 2].at[
                        pl.ds(index // 2 * SHARE, SHARE), pl.ds(1024 * other, 1024)
                    ],
                    out.at[pl.ds(row, SHARE), :],
                    arrived.at[len(copies)],
                )
            )
            copies[-1].start()
    for copy in copies:
        copy.wait()


def left_line(place, parts):
    return pl.pallas_call(
        line_kernel,
        in_specs=[pl.BlockSpec(memory_space=pltpu.SMEM)]
        + [pl.BlockSpec(memory_space=pl.ANY)] * 2,
        out_specs=pl.BlockSpec(memory_space=pltpu.VMEM),
        out_shape=jax.ShapeDtypeStruct((OTHERS, 1024), bf16),
        scratch_shapes=[pltpu.SemaphoreType.DMA((24,))],
        compiler_params=pltpu.CompilerParams(vmem_limit_bytes=40 * 2**20),
        cost_estimate=pl.CostEstimate(
            flops=0, bytes_accessed=4 * OTHERS * 1024, transcendentals=0
        ),
    )(place, *parts)


def update_dot(left, right):
    return lax.dot_general(
        left, right, (((0,), (0,)), ((), ())), preferred_element_type=f32
    )


def plane_sum(count, lefts, lines, right, right_line):
    left = jnp.concatenate([ref[...] for ref in lefts], axis=1)
    line = jnp.concatenate([ref[...] for ref in lines], axis=1)
    return update_dot(left, right[...]) + update_dot(line, right_line[...])


def update_kernel(count, place, *refs):
    lefts, lines = refs[:count], refs[count : 2 * count]
    right, right_line, out = refs[2 * count :]
    total = plane_sum(count, lefts, lines, right, right_line)
    for index in range(count):
        out[index] = total[index * 128 : (index + 1) * 128]


def first_kernel(place, sums, left, line, raw, right, right_1, right_2, right_3, *outs):
    up, down, fitness, scaled, scaled_line = outs

    def total_of(tile):
        return jnp.sum(jnp.sum(tile, axis=1, keepdims=True), axis=0, keepdims=True)

    center = total_of(sums[:4, :]) / POPULATION
    spread = total_of(sums[4:, :]) / POPULATION - center * center
    scale = lax.rsqrt(spread + epsilon)
    fitness[...] = (raw[:4, :] - center) * scale

    def wide(row):
        fit = (raw[row : row + 1, :] - center) * scale / math.sqrt(POPULATION)
        return jnp.transpose(jnp.broadcast_to(fit, (128, 128)))

    def store(target, at, fit, values, row):
        count = fit.shape[0]
        for lane in range(0, 1024, 128):
            drawn = values[row : row + count, lane : lane + 128].astype(f32)
            target[at : at + count, lane : lane + 128] = (fit * drawn).astype(bf16)

    for row in range(4):
        store(scaled, row * 128, wide(row), right, row * 128)
    for index, values in enumerate((right_1, right_2, right_3)):
        for row in range(4):
            fit = wide(4 * index + 4 + row)
            for side in range(2):
                owner = 2 * row + side
                part = fit[side * SHARE : (side + 1) * SHARE]
                store(scaled_line, (3 * owner + index) * SHARE, part, values, owner * SHARE)
    total = plane_sum(1, [left], [line], scaled, scaled_line)
    up[...] = total[:, :512].astype(bf16)
    down[...] = total[:, 512:].astype(bf16)


def left_specs(distances):
    def of(rows, turn):
        return [
            pl.BlockSpec((rows, 128), lambda i, s, dz=dz: (0, turn(lax.rem(s[0] + dz, NZ), s)))
            for dz in distances
        ]

    return of(MEMBERS, lambda z, s: z * NY + s[2]) + of(OTHERS, lambda z, s: z)


def whole(shape):
    return pl.BlockSpec(shape, lambda i, s: (0,) * len(shape))


def update_first(place, sums, left, line, raw, rights):
    shapes = [(MEMBERS, 1024), (OTHERS, 1024)]
    return pl.pallas_call(
        first_kernel,
        grid_spec=pltpu.PrefetchScalarGridSpec(
            num_scalar_prefetch=1,
            grid=(1,),
            in_specs=[whole((8, 128))]
            + left_specs((4,))
            + [whole((16, 128))]
            + [whole((MEMBERS, 1024))] * 4,
            out_specs=[whole((128, 512))] * 2
            + [whole((4, 128))]
            + [whole(shape) for shape in shapes],
        ),
        out_shape=[jax.ShapeDtypeStruct((128, 512), bf16)] * 2
        + [jax.ShapeDtypeStruct((4, 128), f32)]
        + [jax.ShapeDtypeStruct(shape, bf16) for shape in shapes],
        compiler_params=pltpu.CompilerParams(vmem_limit_bytes=40 * 2**20),
        cost_estimate=pl.CostEstimate(
            flops=2 * 2048 * 256 * 512, bytes_accessed=6 * 2**20, transcendentals=0
        ),
    )(place, sums, left, line, raw, *rights)


def update_rest(place, left, line, right, right_line, distances):
    count = len(distances)
    return pl.pallas_call(
        lambda *refs: update_kernel(count, *refs),
        grid_spec=pltpu.PrefetchScalarGridSpec(
            num_scalar_prefetch=1,
            grid=(1,),
            in_specs=left_specs(distances) + [whole((MEMBERS, 1024)), whole((OTHERS, 1024))],
            out_specs=pl.BlockSpec((count, 128, 1024), lambda i, s: (0, 0, 0)),
        ),
        out_shape=jax.ShapeDtypeStruct((count, 128, 1024), f32),
        compiler_params=pltpu.CompilerParams(vmem_limit_bytes=40 * 2**20),
        cost_estimate=pl.CostEstimate(
            flops=2 * 2048 * 256 * 512, bytes_accessed=2**20, transcendentals=0
        ),
    )(place, *[left] * count, *[line] * count, right, right_line)


def shards(inputs, noise_left, noise_right, reward_probe, scores, master):
    pop, wa = lax.axis_index("pop"), lax.axis_index("wa")
    z, y = pop // NY, pop % NY
    half, parity = y // 2, y % 2
    place = jnp.stack([z, parity, y, wa]).astype(jnp.int32)

    weight = master.astype(bf16)
    weight_own = lax.dynamic_slice_in_dim(weight, parity * 512, 512, 1)
    weight_not = lax.dynamic_slice_in_dim(weight, (1 - parity) * 512, 512, 1)
    rel = [
        weight_own,
        swap_pop(weight_not, 1),
        swap_pop(weight_own, 2),
        swap_pop(weight_not, 3),
    ]
    odd, high = parity == 1, half == 1
    rel = [jnp.where(odd, rel[i ^ 1], rel[i]) for i in range(NY)]
    whole_y = jnp.concatenate([jnp.where(high, rel[i ^ 2], rel[i]) for i in range(NY)])

    up1, down1 = move(whole_y, -1, 0), move(whole_y, 1, 0)
    share = lax.dynamic_slice_in_dim(inputs, wa * SHARE, SHARE, 0)
    left_share = lax.dynamic_slice_in_dim(noise_left, wa * SHARE, SHARE, 0)
    left_share = jnp.swapaxes(left_share.reshape(SHARE, NZ, NY, 128), 0, 2).swapaxes(1, 2)
    left_share = left_share.reshape(NY, SHARE, D // NY)
    left_share = [
        lax.dynamic_index_in_dim(left_share, y ^ mask, 0, keepdims=False) for mask in (1, 2, 3)
    ]
    share, left_share, whole_y = lax.optimization_barrier((share, left_share, whole_y))
    share = swap_pop(share, 1)
    lefts = [swap_pop(left_share[k], k + 1) for k in range(3)]
    right_3 = swap_pop(after(noise_right, lefts[1], lefts[2]), 3)
    projected = jnp.sum(inputs.astype(f32) * noise_left.astype(f32), axis=1) / math.sqrt(D)
    projected = projected.reshape(4, 128)

    up1, down1 = lax.optimization_barrier((up1, down1))
    up2, down2 = move(up1, -1, 0), move(down1, 1, 0)
    shares = [after(share, up1, projected)]
    projected = jnp.concatenate([projected, swap_pop(after(projected, up1), 1)])
    shares += [swap_wa(shares[0], 2), None, swap_wa(shares[0], 6)]
    total = forward(place, [inputs], [], [(0, whole_y), (1, up1), (7, down1)])

    up2, down2, total, *lefts = lax.optimization_barrier((up2, down2, total, *lefts))
    up3, down3 = move(up2, -1, 0), move(down2, 1, 0)
    shares[2] = swap_wa(after(shares[0], up2, shares[1], shares[3]), 4)
    right_1 = swap_pop(after(noise_right, up2, right_3, projected), 1)
    crossed = [swap_wa(after(shares[i], up2), 1) if i != 2 else None for i in range(NX)]
    total = forward(place, [inputs], [], [(2, up2), (6, down2)], [total])

    up3, down3, total = lax.optimization_barrier((up3, down3, total))
    far = move(up3, -1, 0)
    crossed[2] = swap_wa(after(shares[2], up3), 1)
    right_2 = swap_pop(after(noise_right, up3, right_1), 2)
    parts = [part for pair in zip(shares, crossed) for part in pair]
    lefts = [after(jnp.concatenate(lefts, axis=1), shares[2])]
    lefts += [swap_wa(lefts[0], 2), None, swap_wa(lefts[0], 6)]
    total, other = forward_both(
        place,
        inputs,
        parts,
        [(0, whole_y), (1, up1), (7, down1), (2, up2), (6, down2), (3, up3), (5, down3)],
        2,
        total,
    )
    lefts[2] = swap_wa(after(lefts[0], lefts[1], lefts[3], other), 4)
    probe = lax.dynamic_slice_in_dim(reward_probe, parity * 512, 512, 0).reshape(1, 512)
    reward = reward_terms(
        place,
        inputs,
        parts,
        [(4, far)],
        total,
        other,
        projected,
        noise_right,
        right_1,
        probe,
    )
    reward = after(reward + swap_wa(reward, 1), lefts[2])
    pair = [swap_wa(reward, mask) for mask in (2, 4, 6)]
    reward = after((reward + pair[0]) + (pair[1] + pair[2]), right_2)
    own = reward[:4] + scores.astype(f32).reshape(4, 128) / 16.0
    reward = jnp.concatenate([own, reward[4:]])
    others = [swap_pop(reward, mask) for mask in (1, 2, 3)]
    line = after(jnp.concatenate(lefts), reward)
    line = left_line(place, [line, swap_wa(line, 1)])
    raw = [
        own + others[0][4:],
        reward[4:] + others[0][:4],
        others[1][:4] + others[2][4:],
        others[1][4:] + others[2][:4],
    ]
    sums = jnp.concatenate(
        [raw[0] + raw[1] + raw[2] + raw[3], sum(tile * tile for tile in raw)]
    )
    sums = sums + move(sums, 1, 0) + move(sums, -1, 0) + move(sums, 2, 0)
    sums = sums + move(sums, 4, 0)

    up, down, fitness, *scaled = update_first(
        place,
        sums,
        noise_left,
        line,
        jnp.concatenate(raw),
        (noise_right, right_1, right_2, right_3),
    )
    up = move(up, 1, 0).astype(f32)
    down = move(down, -1, 0).astype(f32)
    none = jnp.zeros((128, 512), f32)
    up = jnp.concatenate([up, none], axis=1)
    down = jnp.concatenate([none, down], axis=1)
    for distances in ((3, 5), (2, 6), (1, 7, 0)):
        parts = update_rest(place, noise_left, line, *scaled, distances)
        up = move((parts[0] + up).astype(bf16), 1, 0).astype(f32)
        down = move((parts[1] + down).astype(bf16), -1, 0).astype(f32)
    update = parts[2] + up + down
    new_master = master + learn_rate * update
    return (fitness.reshape(MEMBERS), update, new_master, new_master.astype(bf16))


def solution(mesh):
    return jax.shard_map(
        shards,
        mesh=mesh,
        in_specs=(
            P("pop", None),
            P("pop", None),
            P("pop", "wa"),
            P("wa"),
            P("pop"),
            P("pop", "wa"),
        ),
        out_specs=(P("pop"), P("pop", "wa"), P("pop", "wa"), P("pop", "wa")),
        check_vma=False,
    )
```

```python
import math

import jax
import jax.numpy as jnp
from jax import lax
from jax.experimental import pallas as pl
from jax.experimental.pallas import tpu as pltpu
from jax.sharding import PartitionSpec as P

D = 4096
F = 8192
NZ, NY, NX = 8, 4, 4
MEMBERS = 512
POPULATION = MEMBERS * NZ * NY
OTHERS = 3 * MEMBERS
SHARE = 64

noise_scale = 0.5
learn_rate = 0.01
epsilon = 1e-05

bf16 = jnp.bfloat16
f32 = jnp.float32


def move(value, dz, dy):
    pairs = [
        (z * NY + y, (z + dz) % NZ * NY + (y + dy) % NY)
        for z in range(NZ)
        for y in range(NY)
    ]
    return lax.ppermute(value, "pop", pairs)


def swap_pop(value, mask):
    return lax.ppermute(value, "pop", [(i, i ^ mask) for i in range(NZ * NY)])


def swap_wa(value, mask):
    return lax.ppermute(value, "wa", [(i, i ^ mask) for i in range(2 * NX)])


def after(value, *others):
    return lax.optimization_barrier((value, *others))[0]


def load_pieces(place, plan, own, parts, pieces, gathered, weights, arrived):
    copies, at = [], 0
    for (dz, depth), piece in zip(plan, pieces):
        here = pl.ds(at, depth)
        columns = pl.ds(pl.multiple_of(lax.rem(place[0] + dz, NZ) * 512, 512), depth)
        moves = [(piece, weights.at[here, :])]
        for source in own:
            moves.append((source.at[:, columns], gathered.at[pl.ds(0, MEMBERS), here]))
        for index, part in enumerate(parts):
            row = len(own) * MEMBERS + pl.multiple_of((place[3] ^ index) * SHARE, SHARE)
            moves.append((part.at[:, columns], gathered.at[pl.ds(row, SHARE), here]))
        for source, target in moves:
            copies.append(pltpu.make_async_copy(source, target, arrived.at[len(copies)]))
            copies[-1].start()
        at += depth
    return copies


def forward_kernel(plan, counts, place, *refs):
    refs = list(refs)
    own, parts, pieces, totals = [[refs.pop(0) for _ in range(count)] for count in counts]
    out, weights, gathered, arrived = refs
    copies = load_pieces(place, plan, own, parts, pieces, gathered, weights, arrived)
    for copy in copies:
        copy.wait()
    term = jnp.dot(gathered[...], weights[...], preferred_element_type=f32)
    for total in totals:
        term = term + total[...]
    out[...] = term


def forward(place, own, parts, pieces, totals=()):
    plan = tuple((dz, 512) for dz, _ in pieces)
    depth = 512 * len(plan)
    vmem, hbm = pl.BlockSpec(memory_space=pltpu.VMEM), pl.BlockSpec(memory_space=pl.ANY)
    counts = (len(own), len(parts), len(pieces), len(totals))
    return pl.pallas_call(
        lambda *refs: forward_kernel(plan, counts, *refs),
        in_specs=[pl.BlockSpec(memory_space=pltpu.SMEM)]
        + [hbm] * sum(counts[:3])
        + [vmem] * len(totals),
        out_specs=vmem,
        out_shape=jax.ShapeDtypeStruct((MEMBERS, 512), f32),
        scratch_shapes=[
            pltpu.VMEM((depth, 512), bf16),
            pltpu.VMEM((MEMBERS, depth), bf16),
            pltpu.SemaphoreType.DMA(((1 + len(own) + len(parts)) * len(plan),)),
        ],
        compiler_params=pltpu.CompilerParams(vmem_limit_bytes=60 * 2**20),
        cost_estimate=pl.CostEstimate(
            flops=2**20, bytes_accessed=2**16, transcendentals=0
        ),
    )(place, *own, *parts, *[piece for _, piece in pieces], *totals)


def both_kernel(plan, tail, place, inputs, *refs):
    parts, pieces, refs = refs[:8], refs[8 : 8 + len(plan)], refs[8 + len(plan) :]
    total, out_own, out_other, weights, gathered, gathered_own, arrived, arrived_own = refs
    copies = load_pieces(place, plan, [], parts, pieces, gathered, weights, arrived)
    for index, (dz, depth) in enumerate(tail):
        columns = pl.ds(pl.multiple_of(lax.rem(place[0] + dz, NZ) * 512, 512), depth)
        copies.append(
            pltpu.make_async_copy(
                inputs.at[:, columns],
                gathered_own.at[:, pl.ds(index * 512, 512)],
                arrived_own.at[index],
            )
        )
        copies[-1].start()
    for copy in copies:
        copy.wait()
    out_other[...] = jnp.dot(gathered[...], weights[...], preferred_element_type=f32)
    out_own[...] = total[...] + jnp.dot(
        gathered_own[...],
        weights[512 * (len(plan) - len(tail)) :, :],
        preferred_element_type=f32,
    )


def forward_both(place, inputs, parts, pieces, tail, total):
    plan = tuple((dz, 512) for dz, _ in pieces)
    depth = 512 * len(plan)
    vmem, hbm = pl.BlockSpec(memory_space=pltpu.VMEM), pl.BlockSpec(memory_space=pl.ANY)
    return pl.pallas_call(
        lambda *refs: both_kernel(plan, plan[-tail:], *refs),
        in_specs=[pl.BlockSpec(memory_space=pltpu.SMEM)]
        + [hbm] * (9 + len(pieces))
        + [vmem],
        out_specs=[vmem, vmem],
        out_shape=[jax.ShapeDtypeStruct((MEMBERS, 512), f32)] * 2,
        scratch_shapes=[
            pltpu.VMEM((depth, 512), bf16),
            pltpu.VMEM((MEMBERS, depth), bf16),
            pltpu.VMEM((MEMBERS, 512 * tail), bf16),
            pltpu.SemaphoreType.DMA((9 * len(plan),)),
            pltpu.SemaphoreType.DMA((tail,)),
        ],
        compiler_params=pltpu.CompilerParams(vmem_limit_bytes=60 * 2**20),
        cost_estimate=pl.CostEstimate(
            flops=2 * MEMBERS * depth * 512, bytes_accessed=8 * 2**20, transcendentals=0
        ),
    )(place, inputs, *parts, *[piece for _, piece in pieces], total)


def reward_kernel(plan, place, inputs, *refs):
    parts, pieces, refs = refs[:8], refs[8 : 8 + len(plan)], refs[8 + len(plan) :]
    own, other, projected, right, right_1, probe, out, weights, gathered, added, arrived = refs
    copies = load_pieces(
        place, plan, [inputs], parts, pieces, gathered, weights, arrived
    )
    first = pl.multiple_of(place[1] * 512, 512)
    for copy in copies:
        copy.wait()
    for group in range(2 * MEMBERS // 128):
        mine = group < MEMBERS // 128
        total, noise = (own, right) if mine else (other, right_1)
        row = group % (MEMBERS // 128) * 128
        rows = pl.ds(row, 128)
        if row == 0:
            added[...] = jnp.dot(
                gathered[group * 128 : group * 128 + MEMBERS, :],
                weights[...],
                preferred_element_type=f32,
            )
        outputs = total[rows, :] + added[rows, :]
        wide = noise_scale * jnp.transpose(
            jnp.broadcast_to(projected[group : group + 1, :], (128, 128))
        )
        terms = jnp.zeros((128, 128), f32)
        for lane in range(0, 512, 128):
            drawn = noise[rows, pl.ds(pl.multiple_of(first + lane, 128), 128)].astype(f32)
            lanes = outputs[:, lane : lane + 128] + wide * drawn
            terms = terms + jnp.tanh(lanes) * probe[:, lane : lane + 128]
        out[pl.ds(group, 1), :] = jnp.sum(
            jnp.transpose(terms), axis=0, keepdims=True
        ) / math.sqrt(F)


def reward_terms(place, inputs, parts, pieces, *operands):
    plan = tuple((dz, 512) for dz, _ in pieces)
    depth = 512 * len(plan)
    vmem, hbm = pl.BlockSpec(memory_space=pltpu.VMEM), pl.BlockSpec(memory_space=pl.ANY)
    return pl.pallas_call(
        lambda *refs: reward_kernel(plan, *refs),
        in_specs=[pl.BlockSpec(memory_space=pltpu.SMEM)]
        + [hbm] * (9 + len(plan))
        + [vmem] * len(operands),
        out_specs=vmem,
        out_shape=jax.ShapeDtypeStruct((8, 128), f32),
        scratch_shapes=[
            pltpu.VMEM((depth, 512), bf16),
            pltpu.VMEM((2 * MEMBERS, depth), bf16),
            pltpu.VMEM((MEMBERS, 512), f32),
            pltpu.SemaphoreType.DMA((10 * len(plan),)),
        ],
        compiler_params=pltpu.CompilerParams(vmem_limit_bytes=60 * 2**20),
        cost_estimate=pl.CostEstimate(
            flops=4 * MEMBERS * depth * 512, bytes_accessed=6 * 2**20, transcendentals=0
        ),
    )(place, inputs, *parts, *[piece for _, piece in pieces], *operands)


def line_kernel(place, *refs):
    parts, out, arrived = refs[:2], refs[2], refs[3]
    copies = []
    for index in range(2 * NX):
        for other in range(3):
            row = pl.multiple_of((3 * (place[3] ^ index) + other) * SHARE, SHARE)
            copies.append(
                pltpu.make_async_copy(
                    parts[index % 2].at[
                        pl.ds(index // 2 * SHARE, SHARE), pl.ds(1024 * other, 1024)
                    ],
                    out.at[pl.ds(row, SHARE), :],
                    arrived.at[len(copies)],
                )
            )
            copies[-1].start()
    for copy in copies:
        copy.wait()


def left_line(place, parts):
    return pl.pallas_call(
        line_kernel,
        in_specs=[pl.BlockSpec(memory_space=pltpu.SMEM)]
        + [pl.BlockSpec(memory_space=pl.ANY)] * 2,
        out_specs=pl.BlockSpec(memory_space=pltpu.VMEM),
        out_shape=jax.ShapeDtypeStruct((OTHERS, 1024), bf16),
        scratch_shapes=[pltpu.SemaphoreType.DMA((24,))],
        compiler_params=pltpu.CompilerParams(vmem_limit_bytes=40 * 2**20),
        cost_estimate=pl.CostEstimate(
            flops=0, bytes_accessed=4 * OTHERS * 1024, transcendentals=0
        ),
    )(place, *parts)


def update_dot(left, right):
    return lax.dot_general(
        left, right, (((0,), (0,)), ((), ())), preferred_element_type=f32
    )


def plane_sum(count, lefts, lines, right, right_line):
    left = jnp.concatenate([ref[...] for ref in lefts], axis=1)
    line = jnp.concatenate([ref[...] for ref in lines], axis=1)
    return update_dot(left, right[...]) + update_dot(line, right_line[...])


def update_kernel(count, place, *refs):
    lefts, lines = refs[:count], refs[count : 2 * count]
    right, right_line, out = refs[2 * count :]
    total = plane_sum(count, lefts, lines, right, right_line)
    for index in range(count):
        out[index] = total[index * 128 : (index + 1) * 128]


def first_kernel(place, sums, left, line, raw, right, right_1, right_2, right_3, *outs):
    up, down, fitness, scaled, scaled_line = outs

    def total_of(tile):
        return jnp.sum(jnp.sum(tile, axis=1, keepdims=True), axis=0, keepdims=True)

    center = total_of(sums[:4, :]) / POPULATION
    spread = total_of(sums[4:, :]) / POPULATION - center * center
    scale = lax.rsqrt(spread + epsilon)
    fitness[...] = (raw[:4, :] - center) * scale

    def wide(row):
        fit = (raw[row : row + 1, :] - center) * scale / math.sqrt(POPULATION)
        return jnp.transpose(jnp.broadcast_to(fit, (128, 128)))

    def store(target, at, fit, values, row):
        count = fit.shape[0]
        for lane in range(0, 1024, 128):
            drawn = values[row : row + count, lane : lane + 128].astype(f32)
            target[at : at + count, lane : lane + 128] = (fit * drawn).astype(bf16)

    for row in range(4):
        store(scaled, row * 128, wide(row), right, row * 128)
    for index, values in enumerate((right_1, right_2, right_3)):
        for row in range(4):
            fit = wide(4 * index + 4 + row)
            for side in range(2):
                owner = 2 * row + side
                part = fit[side * SHARE : (side + 1) * SHARE]
                store(scaled_line, (3 * owner + index) * SHARE, part, values, owner * SHARE)
    total = plane_sum(1, [left], [line], scaled, scaled_line)
    up[...] = total[:, :512].astype(bf16)
    down[...] = total[:, 512:].astype(bf16)


def left_specs(distances):
    def of(rows, turn):
        return [
            pl.BlockSpec((rows, 128), lambda i, s, dz=dz: (0, turn(lax.rem(s[0] + dz, NZ), s)))
            for dz in distances
        ]

    return of(MEMBERS, lambda z, s: z * NY + s[2]) + of(OTHERS, lambda z, s: z)


def whole(shape):
    return pl.BlockSpec(shape, lambda i, s: (0,) * len(shape))


def update_first(place, sums, left, line, raw, rights):
    shapes = [(MEMBERS, 1024), (OTHERS, 1024)]
    return pl.pallas_call(
        first_kernel,
        grid_spec=pltpu.PrefetchScalarGridSpec(
            num_scalar_prefetch=1,
            grid=(1,),
            in_specs=[whole((8, 128))]
            + left_specs((4,))
            + [whole((16, 128))]
            + [whole((MEMBERS, 1024))] * 4,
            out_specs=[whole((128, 512))] * 2
            + [whole((4, 128))]
            + [whole(shape) for shape in shapes],
        ),
        out_shape=[jax.ShapeDtypeStruct((128, 512), bf16)] * 2
        + [jax.ShapeDtypeStruct((4, 128), f32)]
        + [jax.ShapeDtypeStruct(shape, bf16) for shape in shapes],
        compiler_params=pltpu.CompilerParams(vmem_limit_bytes=40 * 2**20),
        cost_estimate=pl.CostEstimate(
            flops=2 * 2048 * 256 * 512, bytes_accessed=6 * 2**20, transcendentals=0
        ),
    )(place, sums, left, line, raw, *rights)


def update_rest(place, left, line, right, right_line, distances):
    count = len(distances)
    return pl.pallas_call(
        lambda *refs: update_kernel(count, *refs),
        grid_spec=pltpu.PrefetchScalarGridSpec(
            num_scalar_prefetch=1,
            grid=(1,),
            in_specs=left_specs(distances) + [whole((MEMBERS, 1024)), whole((OTHERS, 1024))],
            out_specs=pl.BlockSpec((count, 128, 1024), lambda i, s: (0, 0, 0)),
        ),
        out_shape=jax.ShapeDtypeStruct((count, 128, 1024), f32),
        compiler_params=pltpu.CompilerParams(vmem_limit_bytes=40 * 2**20),
        cost_estimate=pl.CostEstimate(
            flops=2 * 2048 * 256 * 512, bytes_accessed=2**20, transcendentals=0
        ),
    )(place, *[left] * count, *[line] * count, right, right_line)


def shards(inputs, noise_left, noise_right, reward_probe, scores, master):
    pop, wa = lax.axis_index("pop"), lax.axis_index("wa")
    z, y = pop // NY, pop % NY
    half, parity = y // 2, y % 2
    place = jnp.stack([z, parity, y, wa]).astype(jnp.int32)

    weight = master.astype(bf16)
    weight_own = lax.dynamic_slice_in_dim(weight, parity * 512, 512, 1)
    weight_not = lax.dynamic_slice_in_dim(weight, (1 - parity) * 512, 512, 1)
    rel = [
        weight_own,
        swap_pop(weight_not, 1),
        swap_pop(weight_own, 2),
        swap_pop(weight_not, 3),
    ]
    odd, high = parity == 1, half == 1
    rel = [jnp.where(odd, rel[i ^ 1], rel[i]) for i in range(NY)]
    whole_y = jnp.concatenate([jnp.where(high, rel[i ^ 2], rel[i]) for i in range(NY)])

    up1, down1 = move(whole_y, -1, 0), move(whole_y, 1, 0)
    share = lax.dynamic_slice_in_dim(inputs, wa * SHARE, SHARE, 0)
    left_share = lax.dynamic_slice_in_dim(noise_left, wa * SHARE, SHARE, 0)
    left_share = jnp.swapaxes(left_share.reshape(SHARE, NZ, NY, 128), 0, 2).swapaxes(1, 2)
    left_share = left_share.reshape(NY, SHARE, D // NY)
    left_share = [
        lax.dynamic_index_in_dim(left_share, y ^ mask, 0, keepdims=False) for mask in (1, 2, 3)
    ]
    share, left_share, whole_y = lax.optimization_barrier((share, left_share, whole_y))
    share = swap_pop(share, 1)
    lefts = [swap_pop(left_share[k], k + 1) for k in range(3)]
    right_3 = swap_pop(after(noise_right, lefts[1], lefts[2]), 3)
    projected = jnp.sum(inputs.astype(f32) * noise_left.astype(f32), axis=1) / math.sqrt(D)
    projected = projected.reshape(4, 128)

    up1, down1 = lax.optimization_barrier((up1, down1))
    up2, down2 = move(up1, -1, 0), move(down1, 1, 0)
    shares = [after(share, up1, projected)]
    projected = jnp.concatenate([projected, swap_pop(after(projected, up1), 1)])
    shares += [swap_wa(shares[0], 2), None, swap_wa(shares[0], 6)]
    total = forward(place, [inputs], [], [(0, whole_y), (1, up1), (7, down1)])

    up2, down2, total, *lefts = lax.optimization_barrier((up2, down2, total, *lefts))
    up3, down3 = move(up2, -1, 0), move(down2, 1, 0)
    shares[2] = swap_wa(after(shares[0], up2, shares[1], shares[3]), 4)
    right_1 = swap_pop(after(noise_right, up2, right_3, projected), 1)
    crossed = [swap_wa(after(shares[i], up2), 1) if i != 2 else None for i in range(NX)]
    total = forward(place, [inputs], [], [(2, up2), (6, down2)], [total])

    up3, down3, total = lax.optimization_barrier((up3, down3, total))
    far = move(up3, -1, 0)
    crossed[2] = swap_wa(after(shares[2], up3), 1)
    parts = [part for pair in zip(shares, crossed) for part in pair]
    lefts = [after(jnp.concatenate(lefts, axis=1), shares[2])]
    lefts += [swap_wa(lefts[0], 2), None, swap_wa(lefts[0], 6)]
    total, other = forward_both(
        place,
        inputs,
        parts,
        [(0, whole_y), (1, up1), (7, down1), (2, up2), (6, down2), (3, up3), (5, down3)],
        2,
        total,
    )
    right_2 = swap_pop(after(noise_right[:256], right_1, other), 2)
    lefts[2] = swap_wa(after(lefts[0], lefts[1], lefts[3], other), 4)
    probe = lax.dynamic_slice_in_dim(reward_probe, parity * 512, 512, 0).reshape(1, 512)
    reward = reward_terms(
        place,
        inputs,
        parts,
        [(4, far)],
        total,
        other,
        projected,
        noise_right,
        right_1,
        probe,
    )
    reward = after(reward + swap_wa(reward, 1), lefts[2])
    pair = [swap_wa(reward, mask) for mask in (2, 4, 6)]
    reward = after((reward + pair[0]) + (pair[1] + pair[2]), right_2)
    own = reward[:4] + scores.astype(f32).reshape(4, 128) / 16.0
    reward = jnp.concatenate([own, reward[4:]])
    others = [swap_pop(reward, mask) for mask in (1, 2, 3)]
    right_2 = [right_2, swap_pop(after(noise_right[256:], *others), 2)]
    line = after(jnp.concatenate(lefts), reward)
    line = left_line(place, [line, swap_wa(line, 1)])
    raw = [
        own + others[0][4:],
        reward[4:] + others[0][:4],
        others[1][:4] + others[2][4:],
        others[1][4:] + others[2][:4],
    ]
    sums = jnp.concatenate(
        [raw[0] + raw[1] + raw[2] + raw[3], sum(tile * tile for tile in raw)]
    )
    sums = sums + move(sums, 1, 0) + move(sums, -1, 0) + move(sums, 2, 0)
    sums = sums + move(sums, 4, 0)

    up, down, fitness, *scaled = update_first(
        place,
        sums,
        noise_left,
        line,
        jnp.concatenate(raw),
        (noise_right, right_1, jnp.concatenate(right_2), right_3),
    )
    up = move(up, 1, 0).astype(f32)
    down = move(down, -1, 0).astype(f32)
    none = jnp.zeros((128, 512), f32)
    up = jnp.concatenate([up, none], axis=1)
    down = jnp.concatenate([none, down], axis=1)
    for distances in ((3, 5), (2, 6), (1, 7, 0)):
        parts = update_rest(place, noise_left, line, *scaled, distances)
        up = move((parts[0] + up).astype(bf16), 1, 0).astype(f32)
        down = move((parts[1] + down).astype(bf16), -1, 0).astype(f32)
    update = parts[2] + up + down
    new_master = master + learn_rate * update
    return (fitness.reshape(MEMBERS), update, new_master, new_master.astype(bf16))


def solution(mesh):
    return jax.shard_map(
        shards,
        mesh=mesh,
        in_specs=(
            P("pop", None),
            P("pop", None),
            P("pop", "wa"),
            P("wa"),
            P("pop"),
            P("pop", "wa"),
        ),
        out_specs=(P("pop"), P("pop", "wa"), P("pop", "wa"), P("pop", "wa")),
        check_vma=False,
    )
```

```python
import math

import jax
import jax.numpy as jnp
from jax import lax
from jax.experimental import pallas as pl
from jax.experimental.pallas import tpu as pltpu
from jax.sharding import PartitionSpec as P

D = 4096
F = 8192
NZ, NY, NX = 8, 4, 4
MEMBERS = 512
POPULATION = MEMBERS * NZ * NY
OTHERS = 3 * MEMBERS
SHARE = 64

noise_scale = 0.5
learn_rate = 0.01
epsilon = 1e-05

bf16 = jnp.bfloat16
f32 = jnp.float32


def move(value, dz, dy):
    pairs = [
        (z * NY + y, (z + dz) % NZ * NY + (y + dy) % NY)
        for z in range(NZ)
        for y in range(NY)
    ]
    return lax.ppermute(value, "pop", pairs)


def swap_pop(value, mask):
    return lax.ppermute(value, "pop", [(i, i ^ mask) for i in range(NZ * NY)])


def swap_wa(value, mask):
    return lax.ppermute(value, "wa", [(i, i ^ mask) for i in range(2 * NX)])


def after(value, *others):
    return lax.optimization_barrier((value, *others))[0]


def load_pieces(place, plan, own, parts, pieces, gathered, weights, arrived):
    copies, at = [], 0
    for (dz, depth), piece in zip(plan, pieces):
        here = pl.ds(at, depth)
        columns = pl.ds(pl.multiple_of(lax.rem(place[0] + dz, NZ) * 512, 512), depth)
        moves = [(piece, weights.at[here, :])]
        for source in own:
            moves.append((source.at[:, columns], gathered.at[pl.ds(0, MEMBERS), here]))
        for index, part in enumerate(parts):
            row = len(own) * MEMBERS + pl.multiple_of((place[3] ^ index) * SHARE, SHARE)
            moves.append((part.at[:, columns], gathered.at[pl.ds(row, SHARE), here]))
        for source, target in moves:
            copies.append(pltpu.make_async_copy(source, target, arrived.at[len(copies)]))
            copies[-1].start()
        at += depth
    return copies


def forward_kernel(plan, counts, place, *refs):
    refs = list(refs)
    own, parts, pieces, totals = [[refs.pop(0) for _ in range(count)] for count in counts]
    out, weights, gathered, arrived = refs
    copies = load_pieces(place, plan, own, parts, pieces, gathered, weights, arrived)
    for copy in copies:
        copy.wait()
    term = jnp.dot(gathered[...], weights[...], preferred_element_type=f32)
    for total in totals:
        term = term + total[...]
    out[...] = term


def forward(place, own, parts, pieces, totals=()):
    plan = tuple((dz, 512) for dz, _ in pieces)
    depth = 512 * len(plan)
    vmem, hbm = pl.BlockSpec(memory_space=pltpu.VMEM), pl.BlockSpec(memory_space=pl.ANY)
    counts = (len(own), len(parts), len(pieces), len(totals))
    return pl.pallas_call(
        lambda *refs: forward_kernel(plan, counts, *refs),
        in_specs=[pl.BlockSpec(memory_space=pltpu.SMEM)]
        + [hbm] * sum(counts[:3])
        + [vmem] * len(totals),
        out_specs=vmem,
        out_shape=jax.ShapeDtypeStruct((MEMBERS, 512), f32),
        scratch_shapes=[
            pltpu.VMEM((depth, 512), bf16),
            pltpu.VMEM((MEMBERS, depth), bf16),
            pltpu.SemaphoreType.DMA(((1 + len(own) + len(parts)) * len(plan),)),
        ],
        compiler_params=pltpu.CompilerParams(vmem_limit_bytes=60 * 2**20),
        cost_estimate=pl.CostEstimate(
            flops=2**20, bytes_accessed=2**16, transcendentals=0
        ),
    )(place, *own, *parts, *[piece for _, piece in pieces], *totals)


def both_kernel(plan, tail, place, inputs, *refs):
    parts, pieces, refs = refs[:8], refs[8 : 8 + len(plan)], refs[8 + len(plan) :]
    total, out_own, out_other, weights, gathered, gathered_own, arrived, arrived_own = refs
    copies = load_pieces(place, plan, [], parts, pieces, gathered, weights, arrived)
    for index, (dz, depth) in enumerate(tail):
        columns = pl.ds(pl.multiple_of(lax.rem(place[0] + dz, NZ) * 512, 512), depth)
        copies.append(
            pltpu.make_async_copy(
                inputs.at[:, columns],
                gathered_own.at[:, pl.ds(index * 512, 512)],
                arrived_own.at[index],
            )
        )
        copies[-1].start()
    for copy in copies:
        copy.wait()
    out_other[...] = jnp.dot(gathered[...], weights[...], preferred_element_type=f32)
    out_own[...] = total[...] + jnp.dot(
        gathered_own[...],
        weights[512 * (len(plan) - len(tail)) :, :],
        preferred_element_type=f32,
    )


def forward_both(place, inputs, parts, pieces, tail, total):
    plan = tuple((dz, 512) for dz, _ in pieces)
    depth = 512 * len(plan)
    vmem, hbm = pl.BlockSpec(memory_space=pltpu.VMEM), pl.BlockSpec(memory_space=pl.ANY)
    return pl.pallas_call(
        lambda *refs: both_kernel(plan, plan[-tail:], *refs),
        in_specs=[pl.BlockSpec(memory_space=pltpu.SMEM)]
        + [hbm] * (9 + len(pieces))
        + [vmem],
        out_specs=[vmem, vmem],
        out_shape=[jax.ShapeDtypeStruct((MEMBERS, 512), f32)] * 2,
        scratch_shapes=[
            pltpu.VMEM((depth, 512), bf16),
            pltpu.VMEM((MEMBERS, depth), bf16),
            pltpu.VMEM((MEMBERS, 512 * tail), bf16),
            pltpu.SemaphoreType.DMA((9 * len(plan),)),
            pltpu.SemaphoreType.DMA((tail,)),
        ],
        compiler_params=pltpu.CompilerParams(vmem_limit_bytes=60 * 2**20),
        cost_estimate=pl.CostEstimate(
            flops=2 * MEMBERS * depth * 512, bytes_accessed=8 * 2**20, transcendentals=0
        ),
    )(place, inputs, *parts, *[piece for _, piece in pieces], total)


def reward_kernel(plan, place, inputs, *refs):
    parts, pieces, refs = refs[:8], refs[8 : 8 + len(plan)], refs[8 + len(plan) :]
    own, other, projected, right, right_1, probe, out, weights, gathered, added, arrived = refs
    copies = load_pieces(
        place, plan, [inputs], parts, pieces, gathered, weights, arrived
    )
    first = pl.multiple_of(place[1] * 512, 512)
    for copy in copies:
        copy.wait()
    for group in range(2 * MEMBERS // 128):
        mine = group < MEMBERS // 128
        total, noise = (own, right) if mine else (other, right_1)
        row = group % (MEMBERS // 128) * 128
        rows = pl.ds(row, 128)
        if row == 0:
            added[...] = jnp.dot(
                gathered[group * 128 : group * 128 + MEMBERS, :],
                weights[...],
                preferred_element_type=f32,
            )
        outputs = total[rows, :] + added[rows, :]
        wide = noise_scale * jnp.transpose(
            jnp.broadcast_to(projected[group : group + 1, :], (128, 128))
        )
        terms = jnp.zeros((128, 128), f32)
        for lane in range(0, 512, 128):
            drawn = noise[rows, pl.ds(pl.multiple_of(first + lane, 128), 128)].astype(f32)
            lanes = outputs[:, lane : lane + 128] + wide * drawn
            terms = terms + jnp.tanh(lanes) * probe[:, lane : lane + 128]
        out[pl.ds(group, 1), :] = jnp.sum(
            jnp.transpose(terms), axis=0, keepdims=True
        ) / math.sqrt(F)


def reward_terms(place, inputs, parts, pieces, *operands):
    plan = tuple((dz, 512) for dz, _ in pieces)
    depth = 512 * len(plan)
    vmem, hbm = pl.BlockSpec(memory_space=pltpu.VMEM), pl.BlockSpec(memory_space=pl.ANY)
    return pl.pallas_call(
        lambda *refs: reward_kernel(plan, *refs),
        in_specs=[pl.BlockSpec(memory_space=pltpu.SMEM)]
        + [hbm] * (9 + len(plan))
        + [vmem] * len(operands),
        out_specs=vmem,
        out_shape=jax.ShapeDtypeStruct((8, 128), f32),
        scratch_shapes=[
            pltpu.VMEM((depth, 512), bf16),
            pltpu.VMEM((2 * MEMBERS, depth), bf16),
            pltpu.VMEM((MEMBERS, 512), f32),
            pltpu.SemaphoreType.DMA((10 * len(plan),)),
        ],
        compiler_params=pltpu.CompilerParams(vmem_limit_bytes=60 * 2**20),
        cost_estimate=pl.CostEstimate(
            flops=4 * MEMBERS * depth * 512, bytes_accessed=6 * 2**20, transcendentals=0
        ),
    )(place, inputs, *parts, *[piece for _, piece in pieces], *operands)


def line_kernel(place, *refs):
    parts, out, arrived = refs[:2], refs[2], refs[3]
    copies = []
    for index in range(2 * NX):
        for other in range(3):
            row = pl.multiple_of((3 * (place[3] ^ index) + other) * SHARE, SHARE)
            copies.append(
                pltpu.make_async_copy(
                    parts[index % 2].at[
                        pl.ds(index // 2 * SHARE, SHARE), pl.ds(1024 * other, 1024)
                    ],
                    out.at[pl.ds(row, SHARE), :],
                    arrived.at[len(copies)],
                )
            )
            copies[-1].start()
    for copy in copies:
        copy.wait()


def left_line(place, parts):
    return pl.pallas_call(
        line_kernel,
        in_specs=[pl.BlockSpec(memory_space=pltpu.SMEM)]
        + [pl.BlockSpec(memory_space=pl.ANY)] * 2,
        out_specs=pl.BlockSpec(memory_space=pltpu.VMEM),
        out_shape=jax.ShapeDtypeStruct((OTHERS, 1024), bf16),
        scratch_shapes=[pltpu.SemaphoreType.DMA((24,))],
        compiler_params=pltpu.CompilerParams(vmem_limit_bytes=40 * 2**20),
        cost_estimate=pl.CostEstimate(
            flops=0, bytes_accessed=4 * OTHERS * 1024, transcendentals=0
        ),
    )(place, *parts)


def update_dot(left, right):
    return lax.dot_general(
        left, right, (((0,), (0,)), ((), ())), preferred_element_type=f32
    )


def plane_sum(count, lefts, lines, right, right_line):
    left = jnp.concatenate([ref[...] for ref in lefts], axis=1)
    line = jnp.concatenate([ref[...] for ref in lines], axis=1)
    return update_dot(left, right[...]) + update_dot(line, right_line[...])


def update_kernel(count, place, *refs):
    lefts, lines = refs[:count], refs[count : 2 * count]
    right, right_line, out = refs[2 * count :]
    total = plane_sum(count, lefts, lines, right, right_line)
    for index in range(count):
        out[index] = total[index * 128 : (index + 1) * 128]


def first_kernel(place, sums, left, line, raw, right, right_1, right_2, right_3, *outs):
    up, down, fitness, scaled, scaled_line = outs

    def total_of(tile):
        return jnp.sum(jnp.sum(tile, axis=1, keepdims=True), axis=0, keepdims=True)

    center = total_of(sums[:4, :]) / POPULATION
    spread = total_of(sums[4:, :]) / POPULATION - center * center
    scale = lax.rsqrt(spread + epsilon)
    fitness[...] = (raw[:4, :] - center) * scale

    def wide(row):
        fit = (raw[row : row + 1, :] - center) * scale / math.sqrt(POPULATION)
        return jnp.transpose(jnp.broadcast_to(fit, (128, 128)))

    def store(target, at, fit, values, row):
        count = fit.shape[0]
        for lane in range(0, 1024, 128):
            drawn = values[row : row + count, lane : lane + 128].astype(f32)
            target[at : at + count, lane : lane + 128] = (fit * drawn).astype(bf16)

    for row in range(4):
        store(scaled, row * 128, wide(row), right, row * 128)
    for index, values in enumerate((right_1, right_2, right_3)):
        for row in range(4):
            fit = wide(4 * index + 4 + row)
            for side in range(2):
                owner = 2 * row + side
                part = fit[side * SHARE : (side + 1) * SHARE]
                store(scaled_line, (3 * owner + index) * SHARE, part, values, owner * SHARE)
    total = plane_sum(1, [left], [line], scaled, scaled_line)
    up[...] = total[:, :512].astype(bf16)
    down[...] = total[:, 512:].astype(bf16)


def left_specs(distances):
    def of(rows, turn):
        return [
            pl.BlockSpec((rows, 128), lambda i, s, dz=dz: (0, turn(lax.rem(s[0] + dz, NZ), s)))
            for dz in distances
        ]

    return of(MEMBERS, lambda z, s: z * NY + s[2]) + of(OTHERS, lambda z, s: z)


def whole(shape):
    return pl.BlockSpec(shape, lambda i, s: (0,) * len(shape))


def update_first(place, sums, left, line, raw, rights):
    shapes = [(MEMBERS, 1024), (OTHERS, 1024)]
    return pl.pallas_call(
        first_kernel,
        grid_spec=pltpu.PrefetchScalarGridSpec(
            num_scalar_prefetch=1,
            grid=(1,),
            in_specs=[whole((8, 128))]
            + left_specs((4,))
            + [whole((16, 128))]
            + [whole((MEMBERS, 1024))] * 4,
            out_specs=[whole((128, 512))] * 2
            + [whole((4, 128))]
            + [whole(shape) for shape in shapes],
        ),
        out_shape=[jax.ShapeDtypeStruct((128, 512), bf16)] * 2
        + [jax.ShapeDtypeStruct((4, 128), f32)]
        + [jax.ShapeDtypeStruct(shape, bf16) for shape in shapes],
        compiler_params=pltpu.CompilerParams(vmem_limit_bytes=40 * 2**20),
        cost_estimate=pl.CostEstimate(
            flops=2 * 2048 * 256 * 512, bytes_accessed=6 * 2**20, transcendentals=0
        ),
    )(place, sums, left, line, raw, *rights)


def update_rest(place, left, line, right, right_line, distances):
    count = len(distances)
    return pl.pallas_call(
        lambda *refs: update_kernel(count, *refs),
        grid_spec=pltpu.PrefetchScalarGridSpec(
            num_scalar_prefetch=1,
            grid=(1,),
            in_specs=left_specs(distances) + [whole((MEMBERS, 1024)), whole((OTHERS, 1024))],
            out_specs=pl.BlockSpec((count, 128, 1024), lambda i, s: (0, 0, 0)),
        ),
        out_shape=jax.ShapeDtypeStruct((count, 128, 1024), f32),
        compiler_params=pltpu.CompilerParams(vmem_limit_bytes=40 * 2**20),
        cost_estimate=pl.CostEstimate(
            flops=2 * 2048 * 256 * 512, bytes_accessed=2**20, transcendentals=0
        ),
    )(place, *[left] * count, *[line] * count, right, right_line)


def shards(inputs, noise_left, noise_right, reward_probe, scores, master):
    pop, wa = lax.axis_index("pop"), lax.axis_index("wa")
    z, y = pop // NY, pop % NY
    half, parity = y // 2, y % 2
    place = jnp.stack([z, parity, y, wa]).astype(jnp.int32)

    weight = master.astype(bf16)
    weight_own = lax.dynamic_slice_in_dim(weight, parity * 512, 512, 1)
    weight_not = lax.dynamic_slice_in_dim(weight, (1 - parity) * 512, 512, 1)
    rel = [
        weight_own,
        swap_pop(weight_not, 1),
        swap_pop(weight_own, 2),
        swap_pop(weight_not, 3),
    ]
    odd, high = parity == 1, half == 1
    rel = [jnp.where(odd, rel[i ^ 1], rel[i]) for i in range(NY)]
    whole_y = jnp.concatenate([jnp.where(high, rel[i ^ 2], rel[i]) for i in range(NY)])

    up1, down1 = move(whole_y, -1, 0), move(whole_y, 1, 0)
    share = lax.dynamic_slice_in_dim(inputs, wa * SHARE, SHARE, 0)
    left_share = lax.dynamic_slice_in_dim(noise_left, wa * SHARE, SHARE, 0)
    left_share = jnp.swapaxes(left_share.reshape(SHARE, NZ, NY, 128), 0, 2).swapaxes(1, 2)
    left_share = left_share.reshape(NY, SHARE, D // NY)
    left_share = [
        lax.dynamic_index_in_dim(left_share, y ^ mask, 0, keepdims=False) for mask in (1, 2, 3)
    ]
    share, left_share, whole_y = lax.optimization_barrier((share, left_share, whole_y))
    share = swap_pop(share, 1)
    lefts = [swap_pop(left_share[k], k + 1) for k in range(3)]
    right_3 = swap_pop(after(noise_right, lefts[1], lefts[2]), 3)
    projected = jnp.sum(inputs.astype(f32) * noise_left.astype(f32), axis=1) / math.sqrt(D)
    projected = projected.reshape(4, 128)

    up1, down1 = lax.optimization_barrier((up1, down1))
    up2, down2 = move(up1, -1, 0), move(down1, 1, 0)
    shares = [after(share, up1, projected)]
    projected = jnp.concatenate([projected, swap_pop(after(projected, up1), 1)])
    shares += [swap_wa(shares[0], 2), None, swap_wa(shares[0], 6)]
    total = forward(place, [inputs], [], [(0, whole_y), (1, up1), (7, down1)])

    up2, down2, total, *lefts = lax.optimization_barrier((up2, down2, total, *lefts))
    up3, down3 = move(up2, -1, 0), move(down2, 1, 0)
    shares[2] = swap_wa(after(shares[0], up2, shares[1], shares[3]), 4)
    right_1 = swap_pop(after(noise_right, up2, right_3, projected), 1)
    crossed = [swap_wa(after(shares[i], up2), 1) if i != 2 else None for i in range(NX)]
    total = forward(place, [inputs], [], [(2, up2), (6, down2)], [total])

    up3, down3, total = lax.optimization_barrier((up3, down3, total))
    far = move(up3, -1, 0)
    crossed[2] = swap_wa(after(shares[2], up3), 1)
    parts = [part for pair in zip(shares, crossed) for part in pair]
    lefts = [after(jnp.concatenate(lefts, axis=1), shares[2])]
    lefts += [swap_wa(lefts[0], 2), None, swap_wa(lefts[0], 6)]
    total, other = forward_both(
        place,
        inputs,
        parts,
        [(0, whole_y), (1, up1), (7, down1), (2, up2), (6, down2), (3, up3), (5, down3)],
        2,
        total,
    )
    right_2 = swap_pop(after(noise_right[:256], right_1, other), 2)
    lefts[2] = swap_wa(after(lefts[0], lefts[1], lefts[3], other), 4)
    probe = lax.dynamic_slice_in_dim(reward_probe, parity * 512, 512, 0).reshape(1, 512)
    reward = reward_terms(
        place,
        inputs,
        parts,
        [(4, far)],
        total,
        other,
        projected,
        noise_right,
        right_1,
        probe,
    )
    reward = after(reward + swap_wa(reward, 1), lefts[2], right_2)
    pair = [swap_wa(reward, mask) for mask in (2, 4, 6)]
    reward = (reward + pair[0]) + (pair[1] + pair[2])
    own = reward[:4] + scores.astype(f32).reshape(4, 128) / 16.0
    reward = jnp.concatenate([own, reward[4:]])
    others = [swap_pop(reward, mask) for mask in (1, 2, 3)]
    right_2 = [right_2, swap_pop(after(noise_right[256:], *others), 2)]
    line = after(jnp.concatenate(lefts), reward)
    line = left_line(place, [line, swap_wa(line, 1)])
    raw = [
        own + others[0][4:],
        reward[4:] + others[0][:4],
        others[1][:4] + others[2][4:],
        others[1][4:] + others[2][:4],
    ]
    sums = jnp.concatenate(
        [raw[0] + raw[1] + raw[2] + raw[3], sum(tile * tile for tile in raw)]
    )
    sums = sums + move(sums, 1, 0) + move(sums, -1, 0) + move(sums, 2, 0)
    sums = sums + move(sums, 4, 0)

    up, down, fitness, *scaled = update_first(
        place,
        sums,
        noise_left,
        line,
        jnp.concatenate(raw),
        (noise_right, right_1, jnp.concatenate(right_2), right_3),
    )
    up = move(up, 1, 0).astype(f32)
    down = move(down, -1, 0).astype(f32)
    none = jnp.zeros((128, 512), f32)
    up = jnp.concatenate([up, none], axis=1)
    down = jnp.concatenate([none, down], axis=1)
    for distances in ((3, 5), (2, 6), (1, 7, 0)):
        parts = update_rest(place, noise_left, line, *scaled, distances)
        up = move((parts[0] + up).astype(bf16), 1, 0).astype(f32)
        down = move((parts[1] + down).astype(bf16), -1, 0).astype(f32)
    update = parts[2] + up + down
    new_master = master + learn_rate * update
    return (fitness.reshape(MEMBERS), update, new_master, new_master.astype(bf16))


def solution(mesh):
    return jax.shard_map(
        shards,
        mesh=mesh,
        in_specs=(
            P("pop", None),
            P("pop", None),
            P("pop", "wa"),
            P("wa"),
            P("pop"),
            P("pop", "wa"),
        ),
        out_specs=(P("pop"), P("pop", "wa"), P("pop", "wa"), P("pop", "wa")),
        check_vma=False,
    )
```
